128 devices in a mesh: gz: 32 (over z, x, core), gy: 4 (over y).
Axes of the slice: x: 4, y: 4, z: 4, core: 2. Of those that a mesh axis runs over, the one named last changes fastest.
Arguments:
- excess_warmth: float32 [1536, 6144], P('gz', 'gy'), may hold values from -6 to 6
- pore_moisture: float32 [1536, 6144], P('gz', 'gy'), may hold values from 0.55 to 1
- cement_maturity_degree: float32 [1536, 6144], P('gz', 'gy'), may hold values from 0.05 to 0.85
- parcel_filled_tally: int32 [1536, 48], P('gz', 'gy'), may hold values from 0 to 128
- parcel_keeper_position: int32 [1536, 48], P('gz', 'gy'), may hold values from 0 to 1791, as said below
- layer_pouring_times: int32 [192], replicated, may hold values from 0 to 2000
- voigt_strains_stored: float32 [229376, 8, 128], P(('gz', 'gy')), may hold values from -4 to 4
- micro_tension: float32 [229376, 128], P(('gz', 'gy')), may hold values from 0.5 to 5
Outputs:
- temperature_new: float32 [1536, 6144], P('gz', 'gy')
- humidity_new: float32 [1536, 6144], P('gz', 'gy')
- cement_maturity_after: float32 [1536, 6144], P('gz', 'gy')
- creep_strain: float32 [1536, 6144], P('gz', 'gy')
- voigt_strains_after: float32 [229376, 8, 128], P(('gz', 'gy'))
- micro_tension_after: float32 [229376, 128], P(('gz', 'gy'))
The draws below stay inside these ranges and needn't reach their ends.
Inputs may be any that keep to these rules, and one draw needn't show every extreme that they name: `parcel_keeper_position`: number the devices gz index * 4 + gy index. The 576 blocks on one device carry distinct values; value // 14 is the device that holds the block's creep state. In every draw one device holds the states of exactly 14 blocks of every device.
All inputs are finite; a program needn't handle non-finite values.
Results may differ from the reference program's by a relative error of at most 0.00002.
Values sent between devices are 32-bit elements; how exact they have to be, the bound alone decides.
No kernel may reach another device: no remote copies, remote signals or barrier semaphores. Data moves between devices by JAX's collectives and lax.ppermute only.
A program may use at most 64 MiB of HBM per device.

```python
import math
import jax
import jax.numpy as jnp
from jax import lax

CZ = 48
CY = 32
NX = 48
PARCEL_SITES = 128
KU = 8
SWEEPS = 3
LIFT = 8
VERTICAL_LINES = 1536
LINE_SITES = 6144
PARCELS_PER_LINE = 48
NB = 576
CAP = 14
SLOTS = 1792
ALLSLOTS = 229376
NLIFT = 192
N_GZ = 32
N_GY = 4


def draw_parcel_keeper_position(key, part):
    sources = N_GZ * N_GY
    key_owner, key_perm, key_mix = jax.random.split(key, 3)
    forced = jax.random.randint(key_owner, (), 0, sources)

    def one_source(perm_key, mix_key):
        scores = jax.random.permutation(perm_key, SLOTS).astype(jnp.int32)
        slot_ids = jnp.arange(SLOTS).astype(jnp.int32)
        scores = jnp.where(slot_ids // CAP == forced, -1 - slot_ids % CAP, scores)
        ranking = jnp.argsort(scores, stable=True)[:NB].astype(jnp.int32)
        return ranking[jax.random.permutation(mix_key, NB)]
    chosen = jax.vmap(one_source)(jax.random.split(key_perm, sources), jax.random.split(key_mix, sources))
    layout = chosen.reshape(N_GZ, N_GY, CZ, NB // CZ).transpose(0, 2, 1, 3)
    return layout.reshape(VERTICAL_LINES, PARCELS_PER_LINE).astype(jnp.int32)


def with_ends(array, rng, low, top_value):
    longest = array.shape.index(max(array.shape))
    spots = []
    for shift in (0, 1):
        where = [jax.random.randint(jax.random.fold_in(rng, axis), (), 0, length) for axis, length in enumerate(array.shape)]
        where[longest] = (where[longest] + shift) % array.shape[longest]
        spots.append(tuple(where))
    return array.at[spots[0]].set(low).at[spots[1]].set(top_value)


def block_scale(stream_key, shape, cuts, smallest, largest):
    def one(dim, shards_of):
        draws = jax.random.uniform(jax.random.fold_in(jax.random.fold_in(stream_key, 6), dim), (shards_of,), jnp.float32, smallest / len(cuts), largest / len(cuts))
        return jnp.repeat(jnp.exp(draws), shape[dim] // shards_of).reshape((-1,) + (1,) * (len(shape) - dim - 1))

    factor_of = one(*cuts[0])
    for cut in cuts[1:]:
        factor_of = factor_of * one(*cut)
    return factor_of


def normal_values(stream_key, extent, spread, limit, cuts=(), held_as=jnp.bfloat16):
    level = block_scale(stream_key, extent, cuts, -0.22, 0.18) if cuts else 1.0
    values = jax.random.normal(stream_key, extent, jnp.float32) * spread * level
    return jnp.minimum(jnp.maximum(values, -limit), limit).astype(held_as)


def setup_inputs(seed: int = 0) -> dict:
    splits = jax.random.split(jax.random.key(seed), 9)
    return {
        "excess_warmth": normal_values(splits[0], (VERTICAL_LINES, LINE_SITES), 1.0, 6.0, ((0, 32), (1, 4)), jnp.float32),
        "pore_moisture": jnp.clip(0.55 + 0.45 * jax.random.uniform(splits[1], (VERTICAL_LINES, LINE_SITES), jnp.float32) ** block_scale(splits[1], (VERTICAL_LINES, LINE_SITES), ((0, 32), (1, 4)), -0.2, 0.2), 0.55, 1.0),
        "cement_maturity_degree": jnp.clip(0.05 + 0.8 * jax.random.uniform(splits[2], (VERTICAL_LINES, LINE_SITES), jnp.float32) ** block_scale(splits[2], (VERTICAL_LINES, LINE_SITES), ((0, 32), (1, 4)), -0.2, 0.2), 0.05, 0.85),
        "parcel_filled_tally": with_ends(jax.random.randint(splits[3], (VERTICAL_LINES, PARCELS_PER_LINE), 0, PARCEL_SITES + 1), jax.random.fold_in(splits[3], 1), 0, PARCEL_SITES).astype(jnp.int32),
        "parcel_keeper_position": draw_parcel_keeper_position(jax.random.fold_in(splits[8], 71), 0),
        "layer_pouring_times": with_ends(jax.random.randint(splits[5], (NLIFT,), 0, 2001), jax.random.fold_in(splits[5], 1), 0, 2000).astype(jnp.int32),
        "voigt_strains_stored": normal_values(splits[6], (ALLSLOTS, KU, PARCEL_SITES), 0.3, 4.0, ((0, 128),), jnp.float32),
        "micro_tension": jnp.clip(jnp.exp(math.log(5.0) - 2.3025851 * jax.random.uniform(splits[7], (ALLSLOTS, PARCEL_SITES), jnp.float32) ** block_scale(splits[7], (ALLSLOTS, PARCEL_SITES), ((0, 128),), -0.2, 0.2)), 0.5, 5.0),
    }


rate_base = 0.05
activation = 0.5
cement_warmth_output = 4.0
desiccation = 0.5
diff_floor = 0.05
humid_scale = 5.0
expansion_factor = 0.5
drying_contraction_factor = 2.0
now_hours = 2400.0
age_scale = 600.0
creep_activation = 0.3
kelvin_amp = 0.15
micro_rate = 0.2
flow_coef = 0.1

def cement_maturing_speed(field_temp, field_hum, degree):
    humid_term = 7.5 - 7.5 * field_hum
    humid_term = humid_term * humid_term
    return rate_base * (1.0 - degree) * jnp.exp(activation * field_temp) / (1.0 + humid_term * humid_term)

def diffusivity(field_hum):
    ratio = humid_scale * (1.0 - field_hum)
    power = ratio * ratio
    power = power * power
    power = power * power
    power = power * power
    return diff_floor + (1.0 - diff_floor) / (1.0 + power)

def smoothing_iteration(present_warmth, present_moisture, excess_warmth, pore_moisture, cement_maturity_degree, warmth_around, moisture_around):
    chemical_progress = cement_maturing_speed(present_warmth, present_moisture, cement_maturity_degree)
    emitted_warmth_total = warmth_around[0] + warmth_around[1] + warmth_around[2] + warmth_around[3] + warmth_around[4] + warmth_around[5]
    warmth_after = (excess_warmth + cement_warmth_output * chemical_progress + emitted_warmth_total) / 7.0
    own_diff = diffusivity(present_moisture)
    conduct = jnp.zeros_like(present_moisture)
    inflow = jnp.zeros_like(present_moisture)
    for neighbour in moisture_around:
        face_diff = 0.5 * (own_diff + diffusivity(neighbour))
        conduct = conduct + face_diff
        inflow = inflow + face_diff * neighbour
    moisture_after = (pore_moisture - desiccation * chemical_progress + inflow) / (1.0 + conduct)
    return (warmth_after, moisture_after)

def viscous_strain_advance(loading_tension, field_temp, field_hum, parcel_maturity, poured_tally, series_prior, micro_tension_before):
    factor = jnp.exp(creep_activation * field_temp) * (0.1 + 0.9 * field_hum * field_hum)
    lifetimes = 0.1 * 3.0 ** jnp.arange(series_prior.shape[-2]).astype(jnp.float32)
    decays = jnp.exp(-factor[..., None, :] / lifetimes[:, None])
    chain_new = decays * series_prior + kelvin_amp * (1.0 - decays) * loading_tension[..., None, :]
    solidify = jnp.sqrt(age_scale / parcel_maturity) + 0.2
    kelvin_part = solidify * lax.optimization_barrier(jnp.sum(chain_new - series_prior, axis=-2))
    prestress_next = micro_tension_before / (1.0 + micro_rate * factor * micro_tension_before)
    flow_part = flow_coef * factor * prestress_next * loading_tension
    position = jnp.arange(loading_tension.shape[-1]).astype(jnp.float32)
    placed = position < poured_tally
    series_result = jnp.where(placed[..., None, :], chain_new, series_prior)
    micro_tension_result = jnp.where(placed, prestress_next, micro_tension_before)
    small_change = jnp.where(placed, kelvin_part + flow_part, jnp.zeros_like(loading_tension))
    return (series_result, micro_tension_result, small_change)

def nearby_sites(values_in):
    col_total = values_in.shape[1]
    padded = jnp.pad(values_in, ((1, 1), (NX, NX)))
    upper_cell = padded[2:, NX:NX + col_total]
    lower_cell = padded[:-2, NX:NX + col_total]
    north_cell = padded[1:-1, 2 * NX:2 * NX + col_total]
    south_cell = padded[1:-1, 0:col_total]
    vertical_index = jnp.arange(col_total) % NX
    east_cell = jnp.where(vertical_index < NX - 1, padded[1:-1, NX + 1:NX + 1 + col_total], jnp.zeros_like(values_in))
    west_cell = jnp.where(vertical_index > 0, padded[1:-1, NX - 1:NX - 1 + col_total], jnp.zeros_like(values_in))
    return (upper_cell, lower_cell, north_cell, south_cell, east_cell, west_cell)

def reference(excess_warmth, pore_moisture, cement_maturity_degree, parcel_filled_tally, parcel_keeper_position, layer_pouring_times, voigt_strains_stored, micro_tension):
    present_warmth = excess_warmth
    present_moisture = pore_moisture
    for sweep_index in range(SWEEPS):
        present_warmth, present_moisture = smoothing_iteration(present_warmth, present_moisture, excess_warmth, pore_moisture, cement_maturity_degree, nearby_sites(present_warmth), nearby_sites(present_moisture))
    cement_maturity_after = cement_maturity_degree + cement_maturing_speed(present_warmth, present_moisture, cement_maturity_degree)
    loading_tension = -cement_maturity_after * (expansion_factor * present_warmth + drying_contraction_factor * (1.0 - present_moisture))
    row_ids = jnp.arange(VERTICAL_LINES).astype(jnp.int32)
    col_ids = jnp.arange(PARCELS_PER_LINE).astype(jnp.int32)
    sources = (row_ids[:, None] // CZ * N_GY + col_ids[None, :] // (CY * NX // PARCEL_SITES)).astype(jnp.int32)
    slot_index = (parcel_keeper_position // CAP * SLOTS + sources * CAP + parcel_keeper_position % CAP).astype(jnp.int32)
    flat_index = slot_index.reshape(-1)
    row_age = now_hours - layer_pouring_times.astype(jnp.float32)[row_ids // LIFT]
    parcel_maturity = jnp.broadcast_to(row_age[:, None, None], (VERTICAL_LINES, PARCELS_PER_LINE, 1))
    poured_tally = parcel_filled_tally.astype(jnp.float32)[..., None]
    series_prior = voigt_strains_stored[flat_index].reshape(VERTICAL_LINES, PARCELS_PER_LINE, KU, PARCEL_SITES)
    micro_tension_before = micro_tension[flat_index].reshape(VERTICAL_LINES, PARCELS_PER_LINE, PARCEL_SITES)
    series_result, micro_tension_result, small_change = viscous_strain_advance(loading_tension.reshape(VERTICAL_LINES, PARCELS_PER_LINE, PARCEL_SITES), present_warmth.reshape(VERTICAL_LINES, PARCELS_PER_LINE, PARCEL_SITES), present_moisture.reshape(VERTICAL_LINES, PARCELS_PER_LINE, PARCEL_SITES), parcel_maturity, poured_tally, series_prior, micro_tension_before)
    voigt_strains_after = voigt_strains_stored.at[flat_index].set(series_result.reshape(-1, KU, PARCEL_SITES))
    micro_tension_after = micro_tension.at[flat_index].set(micro_tension_result.reshape(-1, PARCEL_SITES))
    return (present_warmth, present_moisture, cement_maturity_after, small_change.reshape(VERTICAL_LINES, PARCELS_PER_LINE * PARCEL_SITES), voigt_strains_after, micro_tension_after)
```

```python
import functools
import math

import jax
import jax.numpy as jnp
from jax import lax
from jax.experimental import pallas as pl
from jax.experimental.pallas import tpu as pltpu
from jax.sharding import PartitionSpec as P

NX = 48
LANES = 128
LIFT = 8
CAP = 14
UNITS = 8
ROWS = 48
TILES = 12
COLS = TILES * LANES
WIDE = (TILES + 3) * LANES
OWN = 2 * LANES
SEND = 32
BACK = 16
AGE_ROW = 14

D0 = 0.05 + 0.95 / (1.0 + 5.0**16)

F32 = jnp.float32
VM = pltpu.VMEM
SM = pltpu.SMEM


def rate_of(u, h, a):
    q = 7.5 - 7.5 * h
    q = q * q
    return 0.05 * (1.0 - a) * jnp.exp(0.5 * u) / (1.0 + q * q)


def excess_diffusivity(h):
    p = 5.0 * (1.0 - h)
    p = p * p
    p = p * p
    p = p * p
    p = p * p
    return (0.05 - D0) + 0.95 / (1.0 + p)


def lanes_of(shape):
    return lax.broadcasted_iota(jnp.int32, shape, len(shape) - 1)


def split_position(p):
    owner = lax.shift_right_logical(p * 37450, 19)
    return owner, p - CAP * owner


def pack_y_kernel(ul, ur, hl, hr, al, ar, to_left, to_right):
    lane = lanes_of((ROWS, LANES))
    first, second = slice(0, LANES), slice(LANES, 2 * LANES)
    to_left[0:ROWS, :] = ul[:, first]
    to_left[ROWS : 2 * ROWS, :] = hl[:, first]
    far_u = pltpu.roll(ul[:, second], 96, 1)
    far_h = pltpu.roll(hl[:, second], 112, 1)
    to_left[2 * ROWS : 3 * ROWS, :] = jnp.where(
        lane < 96, al[:, first], jnp.where(lane < 112, far_u, far_h)
    )
    to_right[0:ROWS, :] = ur[:, second]
    to_right[ROWS : 2 * ROWS, :] = hr[:, second]
    far_u = pltpu.roll(ur[:, first], 16, 1)
    far_h = pltpu.roll(hr[:, first], 32, 1)
    to_right[2 * ROWS : 3 * ROWS, :] = jnp.where(
        lane >= 32, ar[:, second], jnp.where(lane < 16, far_u, far_h)
    )


def pack_y(u, h, a):
    left = pl.BlockSpec((ROWS, 2 * LANES), lambda i: (0, 0))
    right = pl.BlockSpec((ROWS, 2 * LANES), lambda i: (0, COLS // (2 * LANES) - 1))
    whole = pl.BlockSpec((3 * ROWS, LANES), lambda i: (0, 0))
    shape = jax.ShapeDtypeStruct((3 * ROWS, LANES), F32)
    return pl.pallas_call(
        pack_y_kernel,
        grid=(1,),
        out_shape=(shape, shape),
        in_specs=[left, right, left, right, left, right],
        out_specs=(whole, whole),
    )(u, u, h, h, a, a)


def side_tiles(from_left, from_right, lo, n):
    lane = lanes_of((n, LANES))
    rows = [slice(f * ROWS + lo, f * ROWS + lo + n) for f in range(3)]
    lx, rx = from_left[rows[2], :], from_right[rows[2], :]
    zero = jnp.zeros((n, LANES), F32)

    def far(left_shift, right_shift):
        return jnp.where(
            lane < 16,
            pltpu.roll(rx, right_shift, 1),
            jnp.where(lane >= 112, pltpu.roll(lx, left_shift, 1), zero),
        )

    return (
        (far(112, 32), from_left[rows[0], :], from_right[rows[0], :]),
        (far(96, 16), from_left[rows[1], :], from_right[rows[1], :]),
        (zero, jnp.where(lane >= 32, lx, zero), jnp.where(lane < 96, rx, zero)),
    )


def pack_z_kernel(u0, u1, h0, h1, a0, a1, from_left, from_right, up, down):
    row = lax.broadcasted_iota(jnp.int32, (8, WIDE), 0)
    for out, (u, h, a), lo, shifts in (
        (up, (u0, h0, a0), 0, (0, 3, 6)),
        (down, (u1, h1, a1), ROWS - 8, (3, 6, 0)),
    ):
        sides = side_tiles(from_left, from_right, lo, 8)
        wide = []
        for field, side, shift in zip((u, h, a), sides, shifts):
            v = jnp.concatenate([side[0], side[1], field[...], side[2]], axis=1)
            wide.append(pltpu.roll(v, shift, 0) if shift else v)
        out[...] = jnp.where(row < 3, wide[0], jnp.where(row < 6, wide[1], wide[2]))


def pack_z(u, h, a, from_left, from_right):
    top = pl.BlockSpec((8, COLS), lambda i: (0, 0))
    bottom = pl.BlockSpec((8, COLS), lambda i: (ROWS // 8 - 1, 0))
    side = pl.BlockSpec((3 * ROWS, LANES), lambda i: (0, 0))
    out = pl.BlockSpec((8, WIDE), lambda i: (0, 0))
    shape = jax.ShapeDtypeStruct((8, WIDE), F32)
    return pl.pallas_call(
        pack_z_kernel,
        grid=(1,),
        out_shape=(shape, shape),
        in_specs=[top, bottom, top, bottom, top, bottom, side, side],
        out_specs=(out, out),
    )(u, u, h, h, a, a, from_left, from_right)


def table_kernel(place, times, keeper, table):
    lane = lanes_of((ROWS, LANES))
    solid = []
    for r in range(ROWS // LIFT):
        age = 2400.0 - jnp.full((LIFT, LANES), times[place[0] * (ROWS // LIFT) + r], jnp.int32).astype(F32)
        solid.append(jnp.sqrt(600.0 / age) + 0.2)
    solid = jnp.concatenate(solid, axis=0)
    owners, slots = [], []
    for j in range(TILES):
        owner, slot = split_position(jnp.broadcast_to(keeper[:, j : j + 1], (ROWS, LANES)))
        owners.append(jnp.where(owner == lane, 1.0, 0.0))
        slots.append(jnp.where(slot == lane, solid, 0.0))
    table[...] = lax.dot_general(
        jnp.concatenate(owners, axis=0),
        jnp.concatenate(slots, axis=0),
        (((0,), (0,)), ((), ())),
        precision=lax.Precision.HIGHEST,
        preferred_element_type=F32,
    )


def solid_table(place, times, keeper):
    return pl.pallas_call(
        table_kernel,
        out_shape=jax.ShapeDtypeStruct((LANES, LANES), F32),
        in_specs=[
            pl.BlockSpec(memory_space=SM),
            pl.BlockSpec(memory_space=SM),
            pl.BlockSpec(memory_space=VM),
        ],
        out_specs=pl.BlockSpec(memory_space=VM),
    )(place, times, keeper)


def sweep_kernel(
    place,
    keeper,
    tally,
    u_in,
    h_in,
    a_in,
    from_left,
    from_right,
    above,
    below,
    table,
    t_out,
    h_out,
    m_out,
    send,
    u_first,
    h_first,
    a_wide,
    fields,
    phi_buf,
    stress_buf,
):
    gz, gy, last_z, last_y = place[0], place[1], place[2], place[3]
    tiles = ROWS // 8 + 1

    send[...] = jnp.zeros_like(send)

    sides = side_tiles(from_left, from_right, 0, ROWS)
    for wide, own, side in zip((u_first, h_first, a_wide), (u_in, h_in, a_in), sides):
        wide[0:ROWS, 0:LANES] = side[0]
        wide[0:ROWS, LANES:OWN] = side[1]
        wide[0:ROWS, OWN : OWN + COLS] = own[...]
        wide[0:ROWS, OWN + COLS : WIDE] = side[2]
    row8 = lax.broadcasted_iota(jnp.int32, (8, WIDE), 0)
    zero = jnp.zeros((8, WIDE), F32)
    top, bottom = above[...], below[...]
    for wide, down_shift, up_shift in ((u_first, 0, 5), (h_first, 5, 2), (a_wide, 2, 0)):
        b = pltpu.roll(bottom, down_shift, 0) if down_shift else bottom
        t = pltpu.roll(top, up_shift, 0) if up_shift else top
        wide[ROWS : ROWS + 8, :] = jnp.where(row8 < 3, b, jnp.where(row8 >= 5, t, zero))

    column = lanes_of((8, WIDE))
    line = lax.rem(column + (16 * NX - OWN), NX)
    not_first, not_last = line != 0, line != NX - 1
    on_left = (column >= 64) & (column < OWN)
    on_own = (column >= OWN) & (column < OWN + COLS)
    left_is, right_is = (gy > 0).astype(jnp.int32), (gy < last_y).astype(jnp.int32)
    above_is, below_is = (gz > 0).astype(jnp.int32), (gz < last_z).astype(jnp.int32)
    inside_columns = jnp.where(on_own, 1, jnp.where(on_left, left_is, right_is))

    def derived(h):
        d = excess_diffusivity(h)
        return d, d * h

    def fill(r, carry):
        rows = pl.ds(pl.multiple_of(r * 8, 8), 8)
        h = h_first[rows, :]
        d, dh = derived(h)
        fields[0, 0, rows, :] = u_first[rows, :]
        fields[0, 1, rows, :] = h
        fields[0, 2, rows, :] = d
        fields[0, 3, rows, :] = dh
        return carry

    lax.fori_loop(0, tiles, fill, 0)

    def step(src, r):
        here = pl.ds(pl.multiple_of(r * 8, 8), 8)
        before = pl.ds(pl.multiple_of(jnp.where(r == 0, tiles - 1, r - 1) * 8, 8), 8)
        after = pl.ds(pl.multiple_of(jnp.where(r == tiles - 1, 0, r + 1) * 8, 8), 8)

        def around(f):
            v = fields[src, f, here, :]
            lower, upper = fields[src, f, before, :], fields[src, f, after, :]
            total = pltpu.roll(jnp.where(row8 == 0, upper, v), 7, 0)
            total = total + pltpu.roll(jnp.where(row8 == 7, lower, v), 1, 0)
            total = total + pltpu.roll(v, WIDE - NX, 1)
            total = total + pltpu.roll(v, NX, 1)
            total = total + pltpu.roll(jnp.where(not_first, v, 0.0), WIDE - 1, 1)
            total = total + pltpu.roll(jnp.where(not_last, v, 0.0), 1, 1)
            return total

        u, h, d = fields[src, 0, here, :], fields[src, 1, here, :], fields[src, 2, here, :]
        r_now = rate_of(u, h, a_wide[here, :])
        u_next = (u_first[here, :] + 4.0 * r_now + around(0)) * (1.0 / 7.0)
        conduct = 3.0 * (d + 2.0 * D0) + 0.5 * around(2)
        inflow = 0.5 * ((d + 2.0 * D0) * around(1) + around(3))
        h_next = (h_first[here, :] - 0.5 * r_now + inflow) / (1.0 + conduct)
        return u_next, h_next

    def middle(src):
        def run(r, carry):
            rows = pl.ds(pl.multiple_of(r * 8, 8), 8)
            u, h = step(src, r)
            own_rows = (r < tiles - 1).astype(jnp.int32)
            below_in, above_in = jnp.maximum(own_rows, below_is), jnp.maximum(own_rows, above_is)
            keep = inside_columns * jnp.where(row8 < 4, below_in, above_in) > 0
            u, h = jnp.where(keep, u, 0.0), jnp.where(keep, h, 0.0)
            d, dh = derived(h)
            fields[1 - src, 0, rows, :] = u
            fields[1 - src, 1, rows, :] = h
            fields[1 - src, 2, rows, :] = d
            fields[1 - src, 3, rows, :] = dh
            return carry

        lax.fori_loop(0, tiles, run, 0)

    middle(0)
    middle(1)

    lane8 = lanes_of((8, LANES))

    def last(r, carry):
        rows = pl.ds(pl.multiple_of(r * 8, 8), 8)
        u, h = step(0, r)
        u, h = u[:, OWN : OWN + COLS], h[:, OWN : OWN + COLS]
        a = a_in[rows, :]
        m = a + rate_of(u, h, a)
        t_out[rows, :] = u
        h_out[rows, :] = h
        m_out[rows, :] = m
        stress = -m * (0.5 * u + 2.0 * (1.0 - h))
        phi = jnp.exp(0.3 * u) * (0.1 + 0.9 * h * h)
        counts = tally[rows, :]
        for j in range(TILES):
            part = slice(j * LANES, (j + 1) * LANES)
            placed = lane8 < jnp.broadcast_to(counts[:, j : j + 1], (8, LANES))
            block_rows = pl.ds(pl.multiple_of(j * ROWS + r * 8, 8), 8)
            phi_buf[block_rows, :] = jnp.where(placed, phi[:, part], 0.0)
            stress_buf[block_rows, :] = stress[:, part]
        return carry

    lax.fori_loop(0, tiles - 1, last, 0)

    for o in range(LANES):
        send[o * SEND + AGE_ROW : o * SEND + AGE_ROW + 1, :] = table[o : o + 1, :]

    def scatter(z, carry):
        for j in range(TILES):
            owner, slot = split_position(keeper[z, j])
            at = owner * SEND + slot
            block = pl.ds(j * ROWS + z, 1)
            send[pl.ds(at, 1), :] = phi_buf[block, :]
            send[pl.ds(at + 16, 1), :] = stress_buf[block, :]
        return carry

    lax.fori_loop(0, ROWS, scatter, 0)


def sweeps(place, keeper, tally, u, h, a, from_left, from_right, above, below, table):
    grid_shape = jax.ShapeDtypeStruct((ROWS, COLS), F32)
    wide = pltpu.VMEM((ROWS + 8, WIDE), F32)
    return pl.pallas_call(
        sweep_kernel,
        out_shape=(grid_shape, grid_shape, grid_shape, jax.ShapeDtypeStruct((LANES * SEND, LANES), F32)),
        in_specs=[pl.BlockSpec(memory_space=SM)] * 2 + [pl.BlockSpec(memory_space=VM)] * 9,
        out_specs=[pl.BlockSpec(memory_space=VM)] * 4,
        scratch_shapes=[
            wide,
            wide,
            wide,
            pltpu.VMEM((2, 4, ROWS + 8, WIDE), F32),
            pltpu.VMEM((TILES * ROWS, LANES), F32),
            pltpu.VMEM((TILES * ROWS, LANES), F32),
        ],
        compiler_params=pltpu.CompilerParams(vmem_limit_bytes=32 * 2**20),
    )(place, keeper, tally, u, h, a, from_left, from_right, above, below, table)


GROUP = 8


def decay_rates():
    unit = lax.broadcasted_iota(jnp.int32, (UNITS, LANES), 0)
    scale = jnp.zeros((UNITS, LANES), F32)
    for m in range(UNITS):
        scale = jnp.where(unit == m, -1.0 / (0.1 * 3.0**m), scale)
    return scale


def unit_change(chain, phi, stress, k, scale):
    row = slice(k, k + 1)
    b = jnp.exp(jnp.broadcast_to(phi[row, :], (UNITS, LANES)) * scale)
    return (1.0 - b) * (jnp.broadcast_to(stress[row, :], (UNITS, LANES)) - chain)


def sum_units(parts):
    row = lax.broadcasted_iota(jnp.int32, (8, LANES), 0)
    low = row < 4
    pairs = []
    for k in range(4):
        x, y = parts[k], parts[k + 4]
        pairs.append(jnp.where(low, x, y) + pltpu.roll(jnp.where(low, y, x), 4, 0))
    for step in (2, 1):
        first = (row & step) == 0
        pairs = [
            jnp.where(
                first,
                pairs[k] + pltpu.roll(pairs[k], 8 - step, 0),
                pairs[k + step] + pltpu.roll(pairs[k + step], step, 0),
            )
            for k in range(step)
        ]
    return pairs[0]


def creep_kernel(got, chain, tension, creep):
    scale = decay_rates()
    diagonal = lanes_of((BACK, LANES)) == lax.broadcasted_iota(jnp.int32, (BACK, LANES), 0)

    def one(s, carry):
        base = pl.multiple_of(s * SEND, SEND)
        phi, stress = got[pl.ds(base, 16), :], got[pl.ds(base + 16, 16), :]
        ages = jnp.broadcast_to(phi[AGE_ROW : AGE_ROW + 1, :], (BACK, LANES))
        solid = jnp.sum(jnp.where(diagonal, ages, 0.0), axis=1, keepdims=True)
        load = 0.15 * stress
        zero = jnp.zeros((UNITS, LANES), F32)
        changes = [unit_change(chain[s * CAP + k], phi, load, k, scale) for k in range(CAP)]
        changes += [zero] * (BACK - CAP)
        total = jnp.concatenate([sum_units(changes[:8]), sum_units(changes[8:])], axis=0)
        rows = pl.ds(pl.multiple_of(s * BACK, BACK), BACK)
        before = tension[rows, :]
        after = before / (1.0 + 0.2 * phi * before)
        creep[rows, :] = solid * total + 0.1 * phi * after * stress
        return carry

    lax.fori_loop(0, GROUP, one, 0)


def state_kernel(got, chain, tension, chain_out, tension_out):
    scale = decay_rates()

    def one(s, carry):
        base = pl.multiple_of(s * SEND, SEND)
        phi, stress = got[pl.ds(base, 16), :], got[pl.ds(base + 16, 16), :]
        load = 0.15 * stress
        for k in range(CAP):
            prior = chain[s * CAP + k]
            chain_out[s * CAP + k] = prior + unit_change(prior, phi, load, k, scale)
        rows = pl.ds(pl.multiple_of(s * BACK, BACK), BACK)
        before = tension[rows, :]
        tension_out[rows, :] = before / (1.0 + 0.2 * phi * before)
        return carry

    lax.fori_loop(0, GROUP, one, 0)


def owner_specs():
    return (
        pl.BlockSpec((GROUP * SEND, LANES), lambda i: (i, 0)),
        pl.BlockSpec((GROUP * CAP, UNITS, LANES), lambda i: (i, 0, 0)),
        pl.BlockSpec((GROUP * BACK, LANES), lambda i: (i, 0)),
    )


def creep_of(got, chain, tension):
    message, states, rows = owner_specs()
    return pl.pallas_call(
        creep_kernel,
        grid=(LANES // GROUP,),
        out_shape=jax.ShapeDtypeStruct((LANES * BACK, LANES), F32),
        in_specs=[message, states, rows],
        out_specs=rows,
        cost_estimate=pl.CostEstimate(flops=20 * chain.size, bytes_accessed=4 * chain.size, transcendentals=chain.size),
    )(got, chain, tension)


def states_of(got, chain, tension):
    message, states, rows = owner_specs()
    return pl.pallas_call(
        state_kernel,
        grid=(LANES // GROUP,),
        out_shape=(
            jax.ShapeDtypeStruct(chain.shape, F32),
            jax.ShapeDtypeStruct((LANES * BACK, LANES), F32),
        ),
        in_specs=[message, states, rows],
        out_specs=(states, rows),
        cost_estimate=pl.CostEstimate(flops=20 * chain.size, bytes_accessed=8 * chain.size, transcendentals=chain.size),
    )(got, chain, tension)


def collect_kernel(keeper, back, out, blocks):
    def line(z, carry):
        for j in range(TILES):
            owner, slot = split_position(keeper[z, j])
            blocks[pl.ds(j * ROWS + z, 1), :] = back[pl.ds(owner * BACK + slot, 1), :]
        return carry

    lax.fori_loop(0, ROWS, line, 0)
    for j in range(TILES):
        out[:, j * LANES : (j + 1) * LANES] = blocks[j * ROWS : (j + 1) * ROWS, :]


def collect(keeper, back):
    return pl.pallas_call(
        collect_kernel,
        out_shape=jax.ShapeDtypeStruct((ROWS, COLS), F32),
        in_specs=[pl.BlockSpec(memory_space=SM), pl.BlockSpec(memory_space=VM)],
        out_specs=pl.BlockSpec(memory_space=VM),
        scratch_shapes=[pltpu.VMEM((TILES * ROWS, LANES), F32)],
    )(keeper, back)


def both_ways(axis, to_lower, to_higher):
    ends = lax.axis_size(axis) - 1
    from_lower = lax.ppermute(to_higher, axis, [(i, i + 1) for i in range(ends)])
    from_higher = lax.ppermute(to_lower, axis, [(i + 1, i) for i in range(ends)])
    return from_lower, from_higher


def exchange(x):
    return lax.all_to_all(x, ("gz", "gy"), split_axis=0, concat_axis=0, tiled=True)


def body(u, h, a, tally, keeper, times, chain, tension):
    ends = [jnp.int32(lax.axis_size(n) - 1) for n in ("gz", "gy")]
    place = jnp.stack([lax.axis_index("gz"), lax.axis_index("gy"), *ends]).astype(jnp.int32)
    to_left, to_right = pack_y(u, h, a)
    from_left, from_right = both_ways("gy", to_left, to_right)
    table = solid_table(place, times, keeper)
    up, down = pack_z(u, h, a, from_left, from_right)
    above, below = both_ways("gz", up, down)
    t_new, h_new, m_new, send = sweeps(place, keeper, tally, u, h, a, from_left, from_right, above, below, table)
    got = exchange(send)
    tension_wide = jnp.pad(tension.reshape(LANES, CAP, LANES), ((0, 0), (0, BACK - CAP), (0, 0))).reshape(-1, LANES)
    creep = creep_of(got, chain, tension_wide)
    back = exchange(creep)
    chain_new, tension_new = states_of(got, chain, tension_wide)
    tension_new = tension_new.reshape(LANES, BACK, LANES)[:, :CAP].reshape(-1, LANES)
    return t_new, h_new, m_new, collect(keeper, back), chain_new, tension_new


def solution(mesh):
    grid = P("gz", "gy")
    owners = ("gz", "gy")
    return jax.shard_map(
        body,
        mesh=mesh,
        in_specs=(grid, grid, grid, grid, grid, P(), P(owners, None, None), P(owners, None)),
        out_specs=(grid, grid, grid, grid, P(owners, None, None), P(owners, None)),
        check_vma=False,
    )
```

```python
import functools
import math

import jax
import jax.numpy as jnp
from jax import lax
from jax.experimental import pallas as pl
from jax.experimental.pallas import tpu as pltpu
from jax.sharding import PartitionSpec as P

NX = 48
LANES = 128
LIFT = 8
CAP = 14
UNITS = 8
ROWS = 48
TILES = 12
COLS = TILES * LANES
WIDE = (TILES + 3) * LANES
OWN = 2 * LANES
SEND = 32
BACK = 16
AGE_ROW = 14

D0 = 0.05 + 0.95 / (1.0 + 5.0**16)

F32 = jnp.float32


def grant(mib):
    return pltpu.CompilerParams(vmem_limit_bytes=mib * 2**20)


def whole_grant(room):
    return pltpu.CompilerParams(vmem_limit_bytes=64 * 2**20 - room)


HBM = pl.BlockSpec(memory_space=pltpu.HBM)
VMEM = pl.BlockSpec(memory_space=pltpu.VMEM)
SMEM = pl.BlockSpec(memory_space=pltpu.SMEM)


def rate_of(u, h, a):
    q = 7.5 - 7.5 * h
    q = q * q
    return 0.05 * (1.0 - a) * jnp.exp(0.5 * u) / (1.0 + q * q)


def excess_diffusivity(h):
    p = 5.0 * (1.0 - h)
    p = p * p
    p = p * p
    p = p * p
    p = p * p
    return (0.05 - D0) + 0.95 / (1.0 + p)


def lanes_of(shape):
    return lax.broadcasted_iota(jnp.int32, shape, len(shape) - 1)


def split_position(p):
    owner = lax.shift_right_logical(p * 37450, 19)
    return owner, p - CAP * owner


def place_of(p, stride):
    return p + (stride - CAP) * lax.shift_right_logical(p * 37450, 19)


def start_all(pairs, sems):
    copies = [pltpu.make_async_copy(src, dst, sems.at[i]) for i, (src, dst) in enumerate(pairs)]
    for copy in copies:
        copy.start()
    return copies


def pack_y_kernel(u, h, a, to_left, to_right, left, right, sems):
    wide = 2 * LANES
    pairs = []
    for f, field in enumerate((u, h, a)):
        pairs.append((field.at[:, 0:wide], left.at[f]))
        pairs.append((field.at[:, COLS - wide : COLS], right.at[f]))
    for copy in start_all(pairs, sems):
        copy.wait()
    lane = lanes_of((ROWS, LANES))
    first, second = slice(0, LANES), slice(LANES, wide)
    to_left[0:ROWS, :] = left[0, :, first]
    to_left[ROWS : 2 * ROWS, :] = left[1, :, first]
    far_u = pltpu.roll(left[0, :, second], 96, 1)
    far_h = pltpu.roll(left[1, :, second], 112, 1)
    to_left[2 * ROWS : 3 * ROWS, :] = jnp.where(
        lane < 96, left[2, :, first], jnp.where(lane < 112, far_u, far_h)
    )
    to_right[0:ROWS, :] = right[0, :, second]
    to_right[ROWS : 2 * ROWS, :] = right[1, :, second]
    far_u = pltpu.roll(right[0, :, first], 16, 1)
    far_h = pltpu.roll(right[1, :, first], 32, 1)
    to_right[2 * ROWS : 3 * ROWS, :] = jnp.where(
        lane >= 32, right[2, :, second], jnp.where(lane < 16, far_u, far_h)
    )


def pack_y(u, h, a):
    shape = jax.ShapeDtypeStruct((3 * ROWS, LANES), F32)
    return pl.pallas_call(
        pack_y_kernel,
        out_shape=(shape, shape),
        in_specs=[HBM] * 3,
        out_specs=(VMEM, VMEM),
        scratch_shapes=[
            pltpu.VMEM((3, ROWS, 2 * LANES), F32),
            pltpu.VMEM((3, ROWS, 2 * LANES), F32),
            pltpu.SemaphoreType.DMA((6,)),
        ],
        compiler_params=whole_grant(288 * 2**10),
    )(u, h, a)


def side_tiles(from_left, from_right, lo, n):
    lane = lanes_of((n, LANES))
    rows = [slice(f * ROWS + lo, f * ROWS + lo + n) for f in range(3)]
    lx, rx = from_left[rows[2], :], from_right[rows[2], :]
    zero = jnp.zeros((n, LANES), F32)

    def far(left_shift, right_shift):
        return jnp.where(
            lane < 16,
            pltpu.roll(rx, right_shift, 1),
            jnp.where(lane >= 112, pltpu.roll(lx, left_shift, 1), zero),
        )

    return (
        (far(112, 32), from_left[rows[0], :], from_right[rows[0], :]),
        (far(96, 16), from_left[rows[1], :], from_right[rows[1], :]),
        (zero, jnp.where(lane >= 32, lx, zero), jnp.where(lane < 96, rx, zero)),
    )


Z_SHIFTS = (("up", 0, (0, 3, 6)), ("down", ROWS - 8, (3, 6, 0)))


def three_fields(fields, shifts):
    u, h, a = [pltpu.roll(v, s, 0) if s else v for v, s in zip(fields, shifts)]
    row = lax.broadcasted_iota(jnp.int32, u.shape, 0)
    return jnp.where(row < 3, u, jnp.where(row < 6, h, a))


def pack_z_kernel(up_own, down_own, from_left, from_right, up, down):
    for out, own, (_, lo, shifts) in zip((up, down), (up_own, down_own), Z_SHIFTS):
        sides = side_tiles(from_left, from_right, lo, 8)
        out[:, OWN : OWN + COLS] = own[...]
        for t, at in enumerate((0, LANES, OWN + COLS)):
            out[:, at : at + LANES] = three_fields([side[t] for side in sides], shifts)


def pack_z(up_own, down_own, from_left, from_right):
    shape = jax.ShapeDtypeStruct((8, WIDE), F32)
    return pl.pallas_call(
        pack_z_kernel,
        out_shape=(shape, shape),
        in_specs=[VMEM] * 4,
        out_specs=(VMEM, VMEM),
        compiler_params=grant(4),
    )(up_own, down_own, from_left, from_right)


def prepare_kernel(place, times, keeper, u, h, a, table, up, down, ends, sems):
    pairs = []
    for f, field in enumerate((u, h, a)):
        pairs.append((field.at[0:8, :], ends.at[0, f]))
        pairs.append((field.at[ROWS - 8 : ROWS, :], ends.at[1, f]))
    copies = start_all(pairs, sems)
    lane = lanes_of((ROWS, LANES))
    solid = []
    for r in range(ROWS // LIFT):
        age = 2400.0 - jnp.full((LIFT, LANES), times[place[0] * (ROWS // LIFT) + r], jnp.int32).astype(F32)
        solid.append(jnp.sqrt(600.0 / age) + 0.2)
    solid = jnp.concatenate(solid, axis=0)
    owners, slots = [], []
    positions = jnp.transpose(keeper[...])
    for j in range(TILES):
        owner, slot = split_position(jnp.broadcast_to(positions[:, j : j + 1], (ROWS, LANES)))
        owners.append(jnp.where(owner == lane, 1.0, 0.0))
        slots.append(jnp.where(slot == lane, solid, 0.0))
    table[...] = lax.dot_general(
        jnp.concatenate(owners, axis=0),
        jnp.concatenate(slots, axis=0),
        (((0,), (0,)), ((), ())),
        precision=lax.Precision.HIGHEST,
        preferred_element_type=F32,
    )
    for copy in copies:
        copy.wait()
    for out, e, (_, _, shifts) in zip((up, down), (0, 1), Z_SHIFTS):
        out[...] = three_fields([ends[e, f] for f in range(3)], shifts)


def prepare(place, times, keeper, u, h, a):
    rows = jax.ShapeDtypeStruct((8, COLS), F32)
    return pl.pallas_call(
        prepare_kernel,
        out_shape=(jax.ShapeDtypeStruct((LANES, LANES), F32), rows, rows),
        in_specs=[SMEM, SMEM, VMEM] + [HBM] * 3,
        out_specs=[VMEM] * 3,
        scratch_shapes=[pltpu.VMEM((2, 3, 8, COLS), F32), pltpu.SemaphoreType.DMA((6,))],
        compiler_params=whole_grant(544 * 2**10),
    )(place, times, keeper, u, h, a)


def sweep_kernel(
    place,
    keeper,
    tally,
    u_in,
    h_in,
    a_in,
    from_left,
    from_right,
    above,
    below,
    table,
    t_hbm,
    h_hbm,
    m_hbm,
    send_hbm,
    u_first,
    h_first,
    a_wide,
    fields,
    phi_buf,
    load_buf,
    tally_buf,
    t_out,
    h_out,
    m_out,
    send,
    sems,
):
    gz, gy, last_z, last_y = place[0], place[1], place[2], place[3]
    tiles = ROWS // 8 + 1

    own_cells = (slice(0, ROWS), slice(OWN, OWN + COLS))
    loads = start_all(
        [(src, wide.at[own_cells]) for src, wide in ((u_in, u_first), (h_in, h_first), (a_in, a_wide))],
        sems,
    )

    send[...] = jnp.zeros_like(send)
    for o in range(LANES):
        send[o * SEND + AGE_ROW : o * SEND + AGE_ROW + 1, :] = table[o : o + 1, :]

    sides = side_tiles(from_left, from_right, 0, ROWS)
    for wide, side in zip((u_first, h_first, a_wide), sides):
        wide[0:ROWS, 0:LANES] = side[0]
        wide[0:ROWS, LANES:OWN] = side[1]
        wide[0:ROWS, OWN + COLS : WIDE] = side[2]
    row8 = lax.broadcasted_iota(jnp.int32, (8, WIDE), 0)
    zero = jnp.zeros((8, WIDE), F32)
    top, bottom = above[...], below[...]
    for wide, down_shift, up_shift in ((u_first, 0, 5), (h_first, 5, 2), (a_wide, 2, 0)):
        b = pltpu.roll(bottom, down_shift, 0) if down_shift else bottom
        t = pltpu.roll(top, up_shift, 0) if up_shift else top
        wide[ROWS : ROWS + 8, :] = jnp.where(row8 < 3, b, jnp.where(row8 >= 5, t, zero))

    column = lanes_of((8, WIDE))
    line = lax.rem(column + (16 * NX - OWN), NX)
    not_first, not_last = line != 0, line != NX - 1
    on_left = (column >= 64) & (column < OWN)
    on_own = (column >= OWN) & (column < OWN + COLS)
    left_is, right_is = (gy > 0).astype(jnp.int32), (gy < last_y).astype(jnp.int32)
    above_is, below_is = (gz > 0).astype(jnp.int32), (gz < last_z).astype(jnp.int32)
    inside_columns = jnp.where(on_own, 1, jnp.where(on_left, left_is, right_is))

    def derived(h):
        d = excess_diffusivity(h)
        return d, d * h

    for copy in loads:
        copy.wait()

    def fill(r, carry):
        rows = pl.ds(pl.multiple_of(r * 8, 8), 8)
        h = h_first[rows, :]
        d, dh = derived(h)
        fields[0, 0, rows, :] = u_first[rows, :]
        fields[0, 1, rows, :] = h
        fields[0, 2, rows, :] = d
        fields[0, 3, rows, :] = dh
        return carry

    lax.fori_loop(0, tiles, fill, 0)

    def step(src, r):
        here = pl.ds(pl.multiple_of(r * 8, 8), 8)
        before = pl.ds(pl.multiple_of(jnp.where(r == 0, tiles - 1, r - 1) * 8, 8), 8)
        after = pl.ds(pl.multiple_of(jnp.where(r == tiles - 1, 0, r + 1) * 8, 8), 8)

        def around(f):
            v = fields[src, f, here, :]
            lower, upper = fields[src, f, before, :], fields[src, f, after, :]
            total = pltpu.roll(jnp.where(row8 == 0, upper, v), 7, 0)
            total = total + pltpu.roll(jnp.where(row8 == 7, lower, v), 1, 0)
            total = total + pltpu.roll(v, WIDE - NX, 1)
            total = total + pltpu.roll(v, NX, 1)
            total = total + pltpu.roll(jnp.where(not_first, v, 0.0), WIDE - 1, 1)
            total = total + pltpu.roll(jnp.where(not_last, v, 0.0), 1, 1)
            return total

        u, h, d = fields[src, 0, here, :], fields[src, 1, here, :], fields[src, 2, here, :]
        r_now = rate_of(u, h, a_wide[here, :])
        u_next = (u_first[here, :] + 4.0 * r_now + around(0)) * (1.0 / 7.0)
        conduct = 3.0 * (d + 2.0 * D0) + 0.5 * around(2)
        inflow = 0.5 * ((d + 2.0 * D0) * around(1) + around(3))
        h_next = (h_first[here, :] - 0.5 * r_now + inflow) / (1.0 + conduct)
        return u_next, h_next

    def middle(src):
        def run(r, carry):
            rows = pl.ds(pl.multiple_of(r * 8, 8), 8)
            u, h = step(src, r)
            own_rows = (r < tiles - 1).astype(jnp.int32)
            below_in, above_in = jnp.maximum(own_rows, below_is), jnp.maximum(own_rows, above_is)
            keep = inside_columns * jnp.where(row8 < 4, below_in, above_in) > 0
            u, h = jnp.where(keep, u, 0.0), jnp.where(keep, h, 0.0)
            d, dh = derived(h)
            fields[1 - src, 0, rows, :] = u
            fields[1 - src, 1, rows, :] = h
            fields[1 - src, 2, rows, :] = d
            fields[1 - src, 3, rows, :] = dh
            return carry

        lax.fori_loop(0, tiles, run, 0)

    middle(0)
    middle(1)

    lane8 = lanes_of((8, LANES))

    counts_t = jnp.transpose(tally[...])
    for r in range(tiles - 1):
        tally_buf[r * 8 : (r + 1) * 8, 0:TILES] = counts_t[r * 8 : (r + 1) * 8, :]

    def last(r, carry):
        rows = pl.ds(pl.multiple_of(r * 8, 8), 8)
        u, h = step(0, r)
        u, h = u[:, OWN : OWN + COLS], h[:, OWN : OWN + COLS]
        a = a_wide[rows, OWN : OWN + COLS]
        m = a + rate_of(u, h, a)
        t_out[rows, :] = u
        h_out[rows, :] = h
        m_out[rows, :] = m
        load = -m * (0.075 * u + 0.3 * (1.0 - h))
        phi = jnp.exp(0.3 * u) * (0.1 + 0.9 * h * h)
        counts = tally_buf[rows, :]
        for j in range(TILES):
            part = slice(j * LANES, (j + 1) * LANES)
            placed = lane8 < jnp.broadcast_to(counts[:, j : j + 1], (8, LANES))
            block_rows = pl.ds(pl.multiple_of(j * ROWS + r * 8, 8), 8)
            phi_buf[block_rows, :] = jnp.where(placed, phi[:, part], 0.0)
            load_buf[block_rows, :] = load[:, part]
        return carry

    lax.fori_loop(0, tiles - 1, last, 0)

    results = start_all([(t_out, t_hbm), (h_out, h_hbm), (m_out, m_hbm)], sems)

    def scatter(z, carry):
        for j in range(TILES):
            at = place_of(keeper[j, z], SEND)
            block = pl.ds(j * ROWS + z, 1)
            send[pl.ds(at, 1), :] = phi_buf[block, :]
            send[pl.ds(at + 16, 1), :] = load_buf[block, :]
        return carry

    lax.fori_loop(0, ROWS, scatter, 0)
    message = pltpu.make_async_copy(send, send_hbm, sems.at[3])
    message.start()
    for copy in results:
        copy.wait()
    message.wait()


def sweeps(place, keeper, tally, u, h, a, from_left, from_right, above, below, table):
    grid_shape = jax.ShapeDtypeStruct((ROWS, COLS), F32)
    wide = pltpu.VMEM((ROWS + 8, WIDE), F32)
    return pl.pallas_call(
        sweep_kernel,
        out_shape=(grid_shape, grid_shape, grid_shape, jax.ShapeDtypeStruct((LANES * SEND, LANES), F32)),
        in_specs=[SMEM, SMEM, VMEM] + [HBM] * 3 + [VMEM] * 5,
        out_specs=[HBM] * 4,
        scratch_shapes=[
            wide,
            wide,
            wide,
            pltpu.VMEM((2, 4, ROWS + 8, WIDE), F32),
            pltpu.VMEM((TILES * ROWS, LANES), F32),
            pltpu.VMEM((TILES * ROWS, LANES), F32),
            pltpu.VMEM((ROWS, LANES), jnp.int32),
            pltpu.VMEM((ROWS, COLS), F32),
            pltpu.VMEM((ROWS, COLS), F32),
            pltpu.VMEM((ROWS, COLS), F32),
            pltpu.VMEM((LANES * SEND, LANES), F32),
            pltpu.SemaphoreType.DMA((4,)),
        ],
        compiler_params=whole_grant(544 * 2**10),
    )(place, keeper, tally, u, h, a, from_left, from_right, above, below, table)


GROUP = 16
PARTS = LANES // GROUP


def decay_rates():
    unit = lax.broadcasted_iota(jnp.int32, (UNITS, LANES), 0)
    scale = jnp.zeros((UNITS, LANES), F32)
    for m in range(UNITS):
        scale = jnp.where(unit == m, -math.log2(math.e) / (0.1 * 3.0**m), scale)
    return scale


def unit_change(prior, got, at, scale):
    phi = jnp.broadcast_to(got[pl.ds(at, 1), :], (UNITS, LANES))
    load = jnp.broadcast_to(got[pl.ds(at + 16, 1), :], (UNITS, LANES))
    return (1.0 - jnp.exp2(phi * scale)) * (load - prior)


def sum_units(parts):
    row = lax.broadcasted_iota(jnp.int32, (8, LANES), 0)
    low = row < 4
    pairs = []
    for k in range(4):
        x, y = parts[k], parts[k + 4]
        pairs.append(jnp.where(low, x, y) + pltpu.roll(jnp.where(low, y, x), 4, 0))
    for step in (2, 1):
        first = (row & step) == 0
        pairs = [
            jnp.where(
                first,
                pairs[k] + pltpu.roll(pairs[k], 8 - step, 0),
                pairs[k + step] + pltpu.roll(pairs[k + step], step, 0),
            )
            for k in range(step)
        ]
    return pairs[0]


def load_states(chain_hbm, tension_hbm, chain, tension, sems):
    n = GROUP * CAP
    pairs = [(tension_hbm, tension.at[0 : LANES * CAP])]
    pairs += [(chain_hbm.at[i * n : (i + 1) * n], chain.at[i * n : (i + 1) * n]) for i in range(PARTS)]
    return start_all(pairs, sems)


def creep_kernel(got, chain_hbm, tension_hbm, creep_hbm, chain, tension, creep, in_sems, out_sems):
    loads = load_states(chain_hbm, tension_hbm, chain, tension, in_sems)
    scale = decay_rates()
    diagonal = lanes_of((BACK, LANES)) == lax.broadcasted_iota(jnp.int32, (BACK, LANES), 0)

    def one(s, carry):
        base = pl.multiple_of(s * SEND, SEND)
        ages = jnp.broadcast_to(got[pl.ds(base + AGE_ROW, 1), :], (BACK, LANES))
        solid = jnp.sum(jnp.where(diagonal, ages, 0.0), axis=1, keepdims=True)
        zero = jnp.zeros((UNITS, LANES), F32)
        changes = [unit_change(chain[s * CAP + k], got, base + k, scale) for k in range(CAP)]
        changes += [zero] * (BACK - CAP)
        total = jnp.concatenate([sum_units(changes[:8]), sum_units(changes[8:])], axis=0)
        rows = pl.ds(pl.multiple_of(s * BACK, BACK), BACK)
        phi, load = got[pl.ds(base, 16), :], got[pl.ds(base + 16, 16), :]
        before = tension[pl.ds(s * CAP, BACK), :]
        after = before / (1.0 + 0.2 * phi * before)
        creep[rows, :] = solid * total + (0.1 / 0.15) * phi * after * load
        return carry

    tension[LANES * CAP :, :] = jnp.ones((BACK, LANES), F32)
    loads[0].wait()
    stores = []
    for i in range(PARTS):
        loads[1 + i].wait()
        lax.fori_loop(i * GROUP, (i + 1) * GROUP, one, 0, unroll=2)
        part = slice(i * GROUP * BACK, (i + 1) * GROUP * BACK)
        stores.append(pltpu.make_async_copy(creep.at[part], creep_hbm.at[part], out_sems.at[i]))
        stores[-1].start()
    for copy in stores:
        copy.wait()


def state_kernel(got, chain_hbm, tension_hbm, chain_new, tension_new, chain, tension, in_sems, out_sems):
    loads = load_states(chain_hbm, tension_hbm, chain, tension, in_sems)
    scale = decay_rates()
    used = lax.broadcasted_iota(jnp.int32, (BACK, LANES), 0) < CAP

    def one(s, carry):
        base = pl.multiple_of(s * SEND, SEND)
        for k in range(CAP):
            prior = chain[s * CAP + k]
            chain[s * CAP + k] = prior + unit_change(prior, got, base + k, scale)
        phi = got[pl.ds(base, 16), :]
        rows = pl.ds(s * CAP, BACK)
        before = tension[rows, :]
        tension[rows, :] = jnp.where(used, before / (1.0 + 0.2 * phi * before), before)
        return carry

    tension[LANES * CAP :, :] = jnp.ones((BACK, LANES), F32)
    loads[0].wait()
    stores = []
    n = GROUP * CAP
    for i in range(PARTS):
        loads[1 + i].wait()
        lax.fori_loop(i * GROUP, (i + 1) * GROUP, one, 0)
        part = slice(i * n, (i + 1) * n)
        stores.append(pltpu.make_async_copy(chain.at[part], chain_new.at[part], out_sems.at[i]))
        stores[-1].start()
    stores.append(pltpu.make_async_copy(tension.at[0 : LANES * CAP], tension_new, out_sems.at[PARTS]))
    stores[-1].start()
    for copy in stores:
        copy.wait()


def owner_scratch(creep):
    return [
        pltpu.VMEM((LANES * CAP, UNITS, LANES), F32),
        pltpu.VMEM((LANES * CAP + BACK, LANES), F32),
        *creep,
        pltpu.SemaphoreType.DMA((PARTS + 1,)),
        pltpu.SemaphoreType.DMA((PARTS + 1,)),
    ]


def creep_of(got, chain, tension):
    shape = (LANES * BACK, LANES)
    return pl.pallas_call(
        creep_kernel,
        out_shape=jax.ShapeDtypeStruct(shape, F32),
        in_specs=[VMEM, HBM, HBM],
        out_specs=HBM,
        scratch_shapes=owner_scratch([pltpu.VMEM(shape, F32)]),
        compiler_params=whole_grant(2560 * 2**10),
        cost_estimate=pl.CostEstimate(flops=20 * chain.size, bytes_accessed=4 * chain.size, transcendentals=chain.size),
    )(got, chain, tension)


def states_of(got, chain, tension):
    return pl.pallas_call(
        state_kernel,
        out_shape=(jax.ShapeDtypeStruct(chain.shape, F32), jax.ShapeDtypeStruct(tension.shape, F32)),
        in_specs=[VMEM, HBM, HBM],
        out_specs=(HBM, HBM),
        scratch_shapes=owner_scratch([]),
        compiler_params=whole_grant(2560 * 2**10),
        cost_estimate=pl.CostEstimate(flops=20 * chain.size, bytes_accessed=8 * chain.size, transcendentals=chain.size),
    )(got, chain, tension)


def collect_kernel(keeper, back, out, blocks):
    def line(z, carry):
        for j in range(TILES):
            at = place_of(keeper[j, z], BACK)
            blocks[pl.ds(j * ROWS + z, 1), :] = back[pl.ds(at, 1), :]
        return carry

    lax.fori_loop(0, ROWS, line, 0)
    for j in range(TILES):
        out[:, j * LANES : (j + 1) * LANES] = blocks[j * ROWS : (j + 1) * ROWS, :]


def collect(keeper, back):
    return pl.pallas_call(
        collect_kernel,
        out_shape=jax.ShapeDtypeStruct((ROWS, COLS), F32),
        in_specs=[SMEM, VMEM],
        out_specs=VMEM,
        scratch_shapes=[pltpu.VMEM((TILES * ROWS, LANES), F32)],
        compiler_params=grant(4),
    )(keeper, back)


def both_ways(axis, to_lower, to_higher):
    ends = lax.axis_size(axis) - 1
    from_lower = lax.ppermute(to_higher, axis, [(i, i + 1) for i in range(ends)])
    from_higher = lax.ppermute(to_lower, axis, [(i + 1, i) for i in range(ends)])
    return from_lower, from_higher


def exchange(x):
    return lax.all_to_all(x, ("gz", "gy"), split_axis=0, concat_axis=0, tiled=True)


def body(u, h, a, tally, keeper, times, chain, tension):
    ends = [jnp.int32(lax.axis_size(n) - 1) for n in ("gz", "gy")]
    place = jnp.stack([lax.axis_index("gz"), lax.axis_index("gy"), *ends]).astype(jnp.int32)
    tally, keeper = tally.T, keeper.T
    to_left, to_right = pack_y(u, h, a)
    from_left, from_right = both_ways("gy", to_left, to_right)
    table, up_own, down_own = prepare(place, times, keeper, u, h, a)
    up, down = pack_z(up_own, down_own, from_left, from_right)
    above, below = both_ways("gz", up, down)
    t_new, h_new, m_new, send = sweeps(place, keeper, tally, u, h, a, from_left, from_right, above, below, table)
    got = exchange(send)
    creep = creep_of(got, chain, tension)
    back = exchange(creep)
    chain_new, tension_new = states_of(got, chain, tension)
    return t_new, h_new, m_new, collect(keeper, back), chain_new, tension_new


def solution(mesh):
    grid = P("gz", "gy")
    owners = ("gz", "gy")
    return jax.shard_map(
        body,
        mesh=mesh,
        in_specs=(grid, grid, grid, grid, grid, P(), P(owners, None, None), P(owners, None)),
        out_specs=(grid, grid, grid, grid, P(owners, None, None), P(owners, None)),
        check_vma=False,
    )
```

```python
import functools
import math

import jax
import jax.numpy as jnp
from jax import lax
from jax.experimental import pallas as pl
from jax.experimental.pallas import tpu as pltpu
from jax.sharding import PartitionSpec as P

NX = 48
LANES = 128
LIFT = 8
CAP = 14
UNITS = 8
ROWS = 48
TILES = 12
COLS = TILES * LANES
WIDE = (TILES + 3) * LANES
OWN = 2 * LANES
SEND = 2 * CAP + 1
BACK = CAP
AGE_ROW = 2 * CAP

D0 = 0.05 + 0.95 / (1.0 + 5.0**16)

F32 = jnp.float32


def grant(mib):
    return pltpu.CompilerParams(vmem_limit_bytes=mib * 2**20)


def whole_grant(room):
    return pltpu.CompilerParams(vmem_limit_bytes=64 * 2**20 - room)


HBM = pl.BlockSpec(memory_space=pltpu.HBM)
VMEM = pl.BlockSpec(memory_space=pltpu.VMEM)
SMEM = pl.BlockSpec(memory_space=pltpu.SMEM)


def rate_of(u, h, a):
    q = 7.5 - 7.5 * h
    q = q * q
    return 0.05 * (1.0 - a) * jnp.exp(0.5 * u) / (1.0 + q * q)


def excess_diffusivity(h):
    p = 5.0 * (1.0 - h)
    p = p * p
    p = p * p
    p = p * p
    p = p * p
    return (0.05 - D0) + 0.95 / (1.0 + p)


def lanes_of(shape):
    return lax.broadcasted_iota(jnp.int32, shape, len(shape) - 1)


def split_position(p):
    owner = lax.shift_right_logical(p * 37450, 19)
    return owner, p - CAP * owner


def place_of(p, stride):
    return p + (stride - CAP) * lax.shift_right_logical(p * 37450, 19)


def start_all(pairs, sems):
    copies = [pltpu.make_async_copy(src, dst, sems.at[i]) for i, (src, dst) in enumerate(pairs)]
    for copy in copies:
        copy.start()
    return copies


Z_SHIFTS = ((0, (0, 3, 6)), (ROWS - 8, (3, 6, 0)))


def three_fields(fields, shifts):
    u, h, a = [pltpu.roll(v, s, 0) if s else v for v, s in zip(fields, shifts)]
    row = lax.broadcasted_iota(jnp.int32, u.shape, 0)
    return jnp.where(row < 3, u, jnp.where(row < 6, h, a))


def pack_y_kernel(u, h, a, to_left, to_right, up, down, left, right, ends, sems):
    wide = 2 * LANES
    pairs = []
    for f, field in enumerate((u, h, a)):
        pairs.append((field.at[:, 0:wide], left.at[f]))
        pairs.append((field.at[:, COLS - wide : COLS], right.at[f]))
        pairs.append((field.at[0:8, :], ends.at[0, f]))
        pairs.append((field.at[ROWS - 8 : ROWS, :], ends.at[1, f]))
    for copy in start_all(pairs, sems):
        copy.wait()
    for out, e, (_, shifts) in zip((up, down), (0, 1), Z_SHIFTS):
        zero = jnp.zeros((8, LANES), F32)
        out[:, 0:LANES], out[:, LANES:OWN], out[:, OWN + COLS : WIDE] = zero, zero, zero
        out[:, OWN : OWN + COLS] = three_fields([ends[e, f] for f in range(3)], shifts)
    lane = lanes_of((ROWS, LANES))
    first, second = slice(0, LANES), slice(LANES, wide)
    to_left[0:ROWS, :] = left[0, :, first]
    to_left[ROWS : 2 * ROWS, :] = left[1, :, first]
    far_u = pltpu.roll(left[0, :, second], 96, 1)
    far_h = pltpu.roll(left[1, :, second], 112, 1)
    to_left[2 * ROWS : 3 * ROWS, :] = jnp.where(
        lane < 96, left[2, :, first], jnp.where(lane < 112, far_u, far_h)
    )
    to_right[0:ROWS, :] = right[0, :, second]
    to_right[ROWS : 2 * ROWS, :] = right[1, :, second]
    far_u = pltpu.roll(right[0, :, first], 16, 1)
    far_h = pltpu.roll(right[1, :, first], 32, 1)
    to_right[2 * ROWS : 3 * ROWS, :] = jnp.where(
        lane >= 32, right[2, :, second], jnp.where(lane < 16, far_u, far_h)
    )


def pack_y(u, h, a):
    shape = jax.ShapeDtypeStruct((3 * ROWS, LANES), F32)
    rows = jax.ShapeDtypeStruct((8, WIDE), F32)
    return pl.pallas_call(
        pack_y_kernel,
        out_shape=(shape, shape, rows, rows),
        in_specs=[HBM] * 3,
        out_specs=[VMEM] * 4,
        scratch_shapes=[
            pltpu.VMEM((3, ROWS, 2 * LANES), F32),
            pltpu.VMEM((3, ROWS, 2 * LANES), F32),
            pltpu.VMEM((2, 3, 8, COLS), F32),
            pltpu.SemaphoreType.DMA((12,)),
        ],
        compiler_params=whole_grant(500 * 2**10),
    )(u, h, a)


def side_tiles(from_left, from_right, lo, n):
    lane = lanes_of((n, LANES))
    rows = [slice(f * ROWS + lo, f * ROWS + lo + n) for f in range(3)]
    lx, rx = from_left[rows[2], :], from_right[rows[2], :]
    zero = jnp.zeros((n, LANES), F32)

    def far(left_shift, right_shift):
        return jnp.where(
            lane < 16,
            pltpu.roll(rx, right_shift, 1),
            jnp.where(lane >= 112, pltpu.roll(lx, left_shift, 1), zero),
        )

    return (
        (far(112, 32), from_left[rows[0], :], from_right[rows[0], :]),
        (far(96, 16), from_left[rows[1], :], from_right[rows[1], :]),
        (zero, jnp.where(lane >= 32, lx, zero), jnp.where(lane < 96, rx, zero)),
    )


def pack_z_kernel(up_own, down_own, from_left, from_right, up, down, edges, sems):
    pairs = []
    for e, (out, (lo, shifts)) in enumerate(zip((up, down), Z_SHIFTS)):
        sides = side_tiles(from_left, from_right, lo, 8)
        for t in range(3):
            edges[e, :, t * LANES : (t + 1) * LANES] = three_fields([side[t] for side in sides], shifts)
        pairs.append((edges.at[e, :, 0:OWN], out.at[:, 0:OWN]))
        pairs.append((edges.at[e, :, OWN : 3 * LANES], out.at[:, OWN + COLS : WIDE]))
    for copy in start_all(pairs, sems):
        copy.wait()


def pack_z(up_own, down_own, from_left, from_right):
    shape = jax.ShapeDtypeStruct((8, WIDE), F32)
    return pl.pallas_call(
        pack_z_kernel,
        out_shape=(shape, shape),
        in_specs=[HBM, HBM, VMEM, VMEM],
        out_specs=(HBM, HBM),
        input_output_aliases={0: 0, 1: 1},
        scratch_shapes=[pltpu.VMEM((2, 8, 3 * LANES), F32), pltpu.SemaphoreType.DMA((4,))],
        compiler_params=whole_grant(200 * 2**10),
    )(up_own, down_own, from_left, from_right)


def table_kernel(times, keeper, table):
    first = lax.axis_index("gz") * (ROWS // LIFT)
    lane = lanes_of((ROWS, LANES))
    solid = []
    for r in range(ROWS // LIFT):
        age = 2400.0 - jnp.full((LIFT, LANES), times[first + r], jnp.int32).astype(F32)
        solid.append(jnp.sqrt(600.0 / age) + 0.2)
    solid = jnp.concatenate(solid, axis=0)
    owners, slots = [], []
    positions = jnp.transpose(keeper[...])
    for j in range(TILES):
        owner, slot = split_position(jnp.broadcast_to(positions[:, j : j + 1], (ROWS, LANES)))
        owners.append(jnp.where(owner == lane, 1.0, 0.0))
        slots.append(jnp.where(slot == lane, solid, 0.0))
    table[...] = lax.dot_general(
        jnp.concatenate(owners, axis=0),
        jnp.concatenate(slots, axis=0),
        (((0,), (0,)), ((), ())),
        precision=lax.Precision.HIGHEST,
        preferred_element_type=F32,
    )


def solid_table(times, keeper):
    return pl.pallas_call(
        table_kernel,
        out_shape=jax.ShapeDtypeStruct((LANES, LANES), F32),
        in_specs=[SMEM, VMEM],
        out_specs=VMEM,
        compiler_params=whole_grant(600 * 2**10),
    )(times, keeper)


def sweep_kernel(
    keeper,
    tally,
    u_in,
    h_in,
    a_in,
    left_hbm,
    right_hbm,
    above_hbm,
    below_hbm,
    table_hbm,
    t_hbm,
    h_hbm,
    m_hbm,
    send_hbm,
    u_first,
    h_first,
    a_wide,
    fields,
    phi_buf,
    load_buf,
    tally_buf,
    t_out,
    h_out,
    m_out,
    send,
    from_left,
    from_right,
    above,
    below,
    table,
    sems,
):
    gz, gy = lax.axis_index("gz"), lax.axis_index("gy")
    last_z, last_y = lax.axis_size("gz") - 1, lax.axis_size("gy") - 1
    tiles = ROWS // 8 + 1

    own_cells = (slice(0, ROWS), slice(OWN, OWN + COLS))
    pairs = [(src, wide.at[own_cells]) for src, wide in ((u_in, u_first), (h_in, h_first), (a_in, a_wide))]
    pairs += [(left_hbm, from_left), (right_hbm, from_right), (above_hbm, above), (below_hbm, below)]
    pairs += [(table_hbm, table)]
    loads = start_all(pairs, sems)

    send[...] = jnp.zeros_like(send)
    for copy in loads:
        copy.wait()
    for o in range(LANES):
        send[o * SEND + AGE_ROW : o * SEND + AGE_ROW + 1, :] = table[o : o + 1, :]

    sides = side_tiles(from_left, from_right, 0, ROWS)
    for wide, side in zip((u_first, h_first, a_wide), sides):
        wide[0:ROWS, 0:LANES] = side[0]
        wide[0:ROWS, LANES:OWN] = side[1]
        wide[0:ROWS, OWN + COLS : WIDE] = side[2]
    row8 = lax.broadcasted_iota(jnp.int32, (8, WIDE), 0)
    zero = jnp.zeros((8, WIDE), F32)
    top, bottom = above[...], below[...]
    for wide, down_shift, up_shift in ((u_first, 0, 5), (h_first, 5, 2), (a_wide, 2, 0)):
        b = pltpu.roll(bottom, down_shift, 0) if down_shift else bottom
        t = pltpu.roll(top, up_shift, 0) if up_shift else top
        wide[ROWS : ROWS + 8, :] = jnp.where(row8 < 3, b, jnp.where(row8 >= 5, t, zero))

    column = lanes_of((8, WIDE))
    line = lax.rem(column + (16 * NX - OWN), NX)
    not_first, not_last = line != 0, line != NX - 1
    on_left = (column >= 64) & (column < OWN)
    on_own = (column >= OWN) & (column < OWN + COLS)
    left_is, right_is = (gy > 0).astype(jnp.int32), (gy < last_y).astype(jnp.int32)
    above_is, below_is = (gz > 0).astype(jnp.int32), (gz < last_z).astype(jnp.int32)
    inside_columns = jnp.where(on_own, 1, jnp.where(on_left, left_is, right_is))

    def fill(r, carry):
        rows = pl.ds(pl.multiple_of(r * 8, 8), 8)
        h = h_first[rows, :]
        fields[0, 0, rows, :] = u_first[rows, :]
        fields[0, 1, rows, :] = h
        fields[0, 2, rows, :] = excess_diffusivity(h)
        for f in range(3):
            fields[1, f, rows, 0:LANES] = jnp.zeros((8, LANES), F32)
        return carry

    lax.fori_loop(0, tiles, fill, 0)

    def step(src, r):
        here = pl.ds(pl.multiple_of(r * 8, 8), 8)
        before = pl.ds(pl.multiple_of(jnp.where(r == 0, tiles - 1, r - 1) * 8, 8), 8)
        after = pl.ds(pl.multiple_of(jnp.where(r == tiles - 1, 0, r + 1) * 8, 8), 8)

        def around(f):
            v = fields[src, f, here, :]
            lower, upper = fields[src, f, before, :], fields[src, f, after, :]
            return (
                pltpu.roll(jnp.where(row8 == 0, upper, v), 7, 0),
                pltpu.roll(jnp.where(row8 == 7, lower, v), 1, 0),
                pltpu.roll(v, WIDE - NX, 1),
                pltpu.roll(v, NX, 1),
                pltpu.roll(jnp.where(not_first, v, 0.0), WIDE - 1, 1),
                pltpu.roll(jnp.where(not_last, v, 0.0), 1, 1),
            )

        u, h, d = fields[src, 0, here, :], fields[src, 1, here, :], fields[src, 2, here, :]
        r_now = rate_of(u, h, a_wide[here, :])
        u_next = (u_first[here, :] + 4.0 * r_now + sum(around(0))) * (1.0 / 7.0)
        hs, ds = around(1), around(2)
        conduct = 3.0 * (d + 2.0 * D0) + 0.5 * sum(ds)
        inflow = 0.5 * ((d + 2.0 * D0) * sum(hs) + sum(x * y for x, y in zip(ds, hs)))
        h_next = (h_first[here, :] - 0.5 * r_now + inflow) / (1.0 + conduct)
        return u_next, h_next

    def middle(src):
        def run(r, carry):
            rows = pl.ds(pl.multiple_of(r * 8, 8), 8)
            u, h = step(src, r)
            own_rows = (r < tiles - 1).astype(jnp.int32)
            below_in, above_in = jnp.maximum(own_rows, below_is), jnp.maximum(own_rows, above_is)
            keep = inside_columns * jnp.where(row8 < 4, below_in, above_in) > 0
            u, h = jnp.where(keep, u, 0.0), jnp.where(keep, h, 0.0)
            d = excess_diffusivity(h)
            for f, v in enumerate((u, h, d)):
                fields[1 - src, f, rows, LANES:WIDE] = v[:, LANES:WIDE]
            return carry

        lax.fori_loop(0, tiles, run, 0)

    middle(0)
    middle(1)

    lane8 = lanes_of((8, LANES))

    counts_t = jnp.transpose(tally[...])
    for r in range(tiles - 1):
        tally_buf[r * 8 : (r + 1) * 8, 0:TILES] = counts_t[r * 8 : (r + 1) * 8, :]

    def last(r, carry):
        rows = pl.ds(pl.multiple_of(r * 8, 8), 8)
        u, h = step(0, r)
        u, h = u[:, OWN : OWN + COLS], h[:, OWN : OWN + COLS]
        a = a_wide[rows, OWN : OWN + COLS]
        m = a + rate_of(u, h, a)
        t_out[rows, :] = u
        h_out[rows, :] = h
        m_out[rows, :] = m
        load = -m * (0.075 * u + 0.3 * (1.0 - h))
        phi = jnp.exp(0.3 * u) * (0.1 + 0.9 * h * h)
        counts = tally_buf[rows, :]
        for j in range(TILES):
            part = slice(j * LANES, (j + 1) * LANES)
            placed = lane8 < jnp.broadcast_to(counts[:, j : j + 1], (8, LANES))
            block_rows = pl.ds(pl.multiple_of(j * ROWS + r * 8, 8), 8)
            phi_buf[block_rows, :] = jnp.where(placed, phi[:, part], 0.0)
            load_buf[block_rows, :] = load[:, part]
        return carry

    lax.fori_loop(0, tiles - 1, last, 0)

    results = start_all([(t_out, t_hbm), (h_out, h_hbm), (m_out, m_hbm)], sems)

    def scatter(z, carry):
        for j in range(TILES):
            at = place_of(keeper[j, z], SEND)
            block = pl.ds(j * ROWS + z, 1)
            send[pl.ds(at, 1), :] = phi_buf[block, :]
            send[pl.ds(at + CAP, 1), :] = load_buf[block, :]
        return carry

    lax.fori_loop(0, ROWS, scatter, 0)
    message = pltpu.make_async_copy(send, send_hbm, sems.at[3])
    message.start()
    for copy in results:
        copy.wait()
    message.wait()


def sweeps(keeper, tally, u, h, a, from_left, from_right, above, below, table):
    grid_shape = jax.ShapeDtypeStruct((ROWS, COLS), F32)
    wide = pltpu.VMEM((ROWS + 8, WIDE), F32)
    return pl.pallas_call(
        sweep_kernel,
        out_shape=(grid_shape, grid_shape, grid_shape, jax.ShapeDtypeStruct((LANES * SEND, LANES), F32)),
        in_specs=[SMEM, VMEM] + [HBM] * 8,
        out_specs=[HBM] * 4,
        scratch_shapes=[
            wide,
            wide,
            wide,
            pltpu.VMEM((2, 3, ROWS + 8, WIDE), F32),
            pltpu.VMEM((TILES * ROWS, LANES), F32),
            pltpu.VMEM((TILES * ROWS, LANES), F32),
            pltpu.VMEM((ROWS, LANES), jnp.int32),
            pltpu.VMEM((ROWS, COLS), F32),
            pltpu.VMEM((ROWS, COLS), F32),
            pltpu.VMEM((ROWS, COLS), F32),
            pltpu.VMEM((LANES * SEND, LANES), F32),
            pltpu.VMEM((3 * ROWS, LANES), F32),
            pltpu.VMEM((3 * ROWS, LANES), F32),
            pltpu.VMEM((8, WIDE), F32),
            pltpu.VMEM((8, WIDE), F32),
            pltpu.VMEM((LANES, LANES), F32),
            pltpu.SemaphoreType.DMA((8,)),
        ],
        compiler_params=whole_grant(400 * 2**10),
    )(keeper, tally, u, h, a, from_left, from_right, above, below, table)


GROUP = 16
PAD = 16
UNROLL = 4
PARTS = LANES // GROUP


def decay_rates():
    unit = lax.broadcasted_iota(jnp.int32, (UNITS, LANES), 0)
    scale = jnp.zeros((UNITS, LANES), F32)
    for m in range(UNITS):
        scale = jnp.where(unit == m, -math.log2(math.e) / (0.1 * 3.0**m), scale)
    return scale


def unit_change(prior, got, at, scale):
    phi = jnp.broadcast_to(got[pl.ds(at, 1), :], (UNITS, LANES))
    load = jnp.broadcast_to(got[pl.ds(at + CAP, 1), :], (UNITS, LANES))
    return (1.0 - jnp.exp2(phi * scale)) * (load - prior)


def sum_units(parts):
    row = lax.broadcasted_iota(jnp.int32, (8, LANES), 0)
    low = row < 4
    pairs = []
    for k in range(4):
        x, y = parts[k], parts[k + 4]
        pairs.append(jnp.where(low, x, y) + pltpu.roll(jnp.where(low, y, x), 4, 0))
    for step in (2, 1):
        first = (row & step) == 0
        pairs = [
            jnp.where(
                first,
                pairs[k] + pltpu.roll(pairs[k], 8 - step, 0),
                pairs[k + step] + pltpu.roll(pairs[k + step], step, 0),
            )
            for k in range(step)
        ]
    return pairs[0]


def load_states(got_hbm, chain_hbm, tension_hbm, got, chain, tension, sems):
    pairs = [(tension_hbm, tension.at[0 : LANES * CAP])]
    for i in range(PARTS):
        for rows, src, dst in ((GROUP * SEND, got_hbm, got), (GROUP * CAP, chain_hbm, chain)):
            part = slice(i * rows, (i + 1) * rows)
            pairs.append((src.at[part], dst.at[part]))
    return start_all(pairs, sems)


def creep_kernel(got_hbm, chain_hbm, tension_hbm, creep_hbm, got, chain, tension, creep, in_sems, out_sems):
    tension[LANES * CAP :, :] = jnp.ones((PAD, LANES), F32)
    loads = load_states(got_hbm, chain_hbm, tension_hbm, got, chain, tension, in_sems)
    scale = decay_rates()
    diagonal = lanes_of((16, LANES)) == lax.broadcasted_iota(jnp.int32, (16, LANES), 0)

    def one(s, carry):
        base = s * SEND
        ages = jnp.broadcast_to(got[pl.ds(base + AGE_ROW, 1), :], (16, LANES))
        solid = jnp.sum(jnp.where(diagonal, ages, 0.0), axis=1, keepdims=True)
        zero = jnp.zeros((UNITS, LANES), F32)
        changes = [unit_change(chain[s * CAP + k], got, base + k, scale) for k in range(CAP)]
        changes += [zero] * (16 - CAP)
        total = jnp.concatenate([sum_units(changes[:8]), sum_units(changes[8:])], axis=0)
        rows = pl.ds(s * CAP, 16)
        phi, load = got[pl.ds(base, 16), :], got[pl.ds(base + CAP - 1, 16), :]
        load = pltpu.roll(load, 15, 0)
        before = tension[rows, :]
        after = before / (1.0 + 0.2 * phi * before)
        creep[rows, :] = solid * total + (0.1 / 0.15) * phi * after * load
        return carry

    loads[0].wait()
    stores = []
    for i in range(PARTS):
        for copy in loads[1 + 2 * i : 3 + 2 * i]:
            copy.wait()
        lax.fori_loop(i * GROUP, (i + 1) * GROUP, one, 0, unroll=UNROLL)
        part = slice(i * GROUP * BACK, (i + 1) * GROUP * BACK)
        stores.append(pltpu.make_async_copy(creep.at[part], creep_hbm.at[part], out_sems.at[i]))
        stores[-1].start()
    for copy in stores:
        copy.wait()


def state_kernel(
    got_hbm, chain_hbm, tension_hbm, chain_new, tension_new, got, chain, tension, in_sems, out_sems
):
    tension[LANES * CAP :, :] = jnp.ones((PAD, LANES), F32)
    loads = load_states(got_hbm, chain_hbm, tension_hbm, got, chain, tension, in_sems)
    scale = decay_rates()
    used = lax.broadcasted_iota(jnp.int32, (16, LANES), 0) < CAP

    def one(s, carry):
        base = s * SEND
        for k in range(CAP):
            prior = chain[s * CAP + k]
            chain[s * CAP + k] = prior + unit_change(prior, got, base + k, scale)
        phi = got[pl.ds(base, 16), :]
        rows = pl.ds(s * CAP, 16)
        before = tension[rows, :]
        tension[rows, :] = jnp.where(used, before / (1.0 + 0.2 * phi * before), before)
        return carry

    loads[0].wait()
    stores = []
    n = GROUP * CAP
    for i in range(PARTS):
        for copy in loads[1 + 2 * i : 3 + 2 * i]:
            copy.wait()
        lax.fori_loop(i * GROUP, (i + 1) * GROUP, one, 0, unroll=2)
        part = slice(i * n, (i + 1) * n)
        stores.append(pltpu.make_async_copy(chain.at[part], chain_new.at[part], out_sems.at[i]))
        stores[-1].start()
    stores.append(pltpu.make_async_copy(tension.at[0 : LANES * CAP], tension_new, out_sems.at[PARTS]))
    stores[-1].start()
    for copy in stores:
        copy.wait()


def owner_scratch(creep):
    return [
        pltpu.VMEM((LANES * SEND, LANES), F32),
        pltpu.VMEM((LANES * CAP, UNITS, LANES), F32),
        pltpu.VMEM((LANES * CAP + PAD, LANES), F32),
        *creep,
        pltpu.SemaphoreType.DMA((2 * PARTS + 1,)),
        pltpu.SemaphoreType.DMA((PARTS + 1,)),
    ]


def creep_of(got, chain, tension):
    shape = (LANES * BACK, LANES)
    return pl.pallas_call(
        creep_kernel,
        out_shape=jax.ShapeDtypeStruct(shape, F32),
        in_specs=[HBM] * 3,
        out_specs=HBM,
        scratch_shapes=owner_scratch([pltpu.VMEM((LANES * CAP + PAD, LANES), F32)]),
        compiler_params=whole_grant(600 * 2**10),
        cost_estimate=pl.CostEstimate(flops=20 * chain.size, bytes_accessed=4 * chain.size, transcendentals=chain.size),
    )(got, chain, tension)


def states_of(got, chain, tension):
    return pl.pallas_call(
        state_kernel,
        out_shape=(jax.ShapeDtypeStruct(chain.shape, F32), jax.ShapeDtypeStruct(tension.shape, F32)),
        in_specs=[HBM] * 3,
        out_specs=(HBM, HBM),
        scratch_shapes=owner_scratch([]),
        compiler_params=whole_grant(600 * 2**10),
        cost_estimate=pl.CostEstimate(flops=20 * chain.size, bytes_accessed=8 * chain.size, transcendentals=chain.size),
    )(got, chain, tension)


def collect_kernel(keeper, back, out, blocks):
    def line(z, carry):
        for j in range(TILES):
            at = place_of(keeper[j, z], BACK)
            blocks[pl.ds(j * ROWS + z, 1), :] = back[pl.ds(at, 1), :]
        return carry

    lax.fori_loop(0, ROWS, line, 0)
    for j in range(TILES):
        out[:, j * LANES : (j + 1) * LANES] = blocks[j * ROWS : (j + 1) * ROWS, :]


def collect(keeper, back):
    return pl.pallas_call(
        collect_kernel,
        out_shape=jax.ShapeDtypeStruct((ROWS, COLS), F32),
        in_specs=[SMEM, VMEM],
        out_specs=VMEM,
        scratch_shapes=[pltpu.VMEM((TILES * ROWS, LANES), F32)],
        compiler_params=grant(4),
    )(keeper, back)


def both_ways(axis, to_lower, to_higher):
    ends = lax.axis_size(axis) - 1
    from_lower = lax.ppermute(to_higher, axis, [(i, i + 1) for i in range(ends)])
    from_higher = lax.ppermute(to_lower, axis, [(i + 1, i) for i in range(ends)])
    return from_lower, from_higher


def exchange(x):
    flat = x.reshape(LANES, 1, -1)
    return lax.all_to_all(flat, ("gz", "gy"), split_axis=0, concat_axis=0, tiled=True).reshape(x.shape)


def body(u, h, a, tally, keeper, times, chain, tension):
    tally, keeper = tally.T, keeper.T
    to_left, to_right, up_own, down_own = pack_y(u, h, a)
    from_left, from_right = both_ways("gy", to_left, to_right)
    table = solid_table(times, keeper)
    up_own, down_own, table = lax.optimization_barrier((up_own, down_own, table))
    up, down = pack_z(up_own, down_own, from_left, from_right)
    above, below = both_ways("gz", up, down)
    t_new, h_new, m_new, send = sweeps(keeper, tally, u, h, a, from_left, from_right, above, below, table)
    got = exchange(send)
    creep = creep_of(got, chain, tension)
    back = exchange(creep)
    chain_new, tension_new = states_of(got, chain, tension)
    return t_new, h_new, m_new, collect(keeper, back), chain_new, tension_new


def solution(mesh):
    grid = P("gz", "gy")
    owners = ("gz", "gy")
    return jax.shard_map(
        body,
        mesh=mesh,
        in_specs=(grid, grid, grid, grid, grid, P(), P(owners, None, None), P(owners, None)),
        out_specs=(grid, grid, grid, grid, P(owners, None, None), P(owners, None)),
        check_vma=False,
    )
```

```python
import functools
import math

import jax
import jax.numpy as jnp
from jax import lax
from jax.experimental import pallas as pl
from jax.experimental.pallas import tpu as pltpu
from jax.sharding import PartitionSpec as P

NX = 48
LANES = 128
LIFT = 8
CAP = 14
UNITS = 8
ROWS = 48
TILES = 12
COLS = TILES * LANES
WIDE = (TILES + 3) * LANES
OWN = 2 * LANES
SEND = 2 * CAP + 1
BACK = CAP
AGE_ROW = 2 * CAP

D0 = 0.05 + 0.95 / (1.0 + 5.0**16)

F32 = jnp.float32


def grant(mib):
    return pltpu.CompilerParams(vmem_limit_bytes=mib * 2**20)


def whole_grant(room):
    return pltpu.CompilerParams(vmem_limit_bytes=64 * 2**20 - room)


HBM = pl.BlockSpec(memory_space=pltpu.HBM)
VMEM = pl.BlockSpec(memory_space=pltpu.VMEM)
SMEM = pl.BlockSpec(memory_space=pltpu.SMEM)


def rate_of(u, h, a):
    q = 7.5 - 7.5 * h
    q = q * q
    return 0.05 * (1.0 - a) * jnp.exp(0.5 * u) / (1.0 + q * q)


def excess_diffusivity(h):
    p = 5.0 * (1.0 - h)
    p = p * p
    p = p * p
    p = p * p
    p = p * p
    return (0.05 - D0) + 0.95 / (1.0 + p)


def lanes_of(shape):
    return lax.broadcasted_iota(jnp.int32, shape, len(shape) - 1)


def split_position(p):
    owner = lax.shift_right_logical(p * 37450, 19)
    return owner, p - CAP * owner


def place_of(p, stride):
    return p + (stride - CAP) * lax.shift_right_logical(p * 37450, 19)


def start_all(pairs, sems):
    copies = [pltpu.make_async_copy(src, dst, sems.at[i]) for i, (src, dst) in enumerate(pairs)]
    for copy in copies:
        copy.start()
    return copies


Z_SHIFTS = ((0, (0, 3, 6)), (ROWS - 8, (3, 6, 0)))


def three_fields(fields, shifts):
    u, h, a = [pltpu.roll(v, s, 0) if s else v for v, s in zip(fields, shifts)]
    row = lax.broadcasted_iota(jnp.int32, u.shape, 0)
    return jnp.where(row < 3, u, jnp.where(row < 6, h, a))


def pack_y_kernel(u, h, a, to_left, to_right, up, down, left, right, ends, sems):
    wide = 2 * LANES
    pairs = []
    for f, field in enumerate((u, h, a)):
        pairs.append((field.at[:, 0:wide], left.at[f]))
        pairs.append((field.at[:, COLS - wide : COLS], right.at[f]))
        pairs.append((field.at[0:8, :], ends.at[0, f]))
        pairs.append((field.at[ROWS - 8 : ROWS, :], ends.at[1, f]))
    for copy in start_all(pairs, sems):
        copy.wait()
    for out, e, (_, shifts) in zip((up, down), (0, 1), Z_SHIFTS):
        zero = jnp.zeros((8, LANES), F32)
        out[:, 0:LANES], out[:, LANES:OWN], out[:, OWN + COLS : WIDE] = zero, zero, zero
        out[:, OWN : OWN + COLS] = three_fields([ends[e, f] for f in range(3)], shifts)
    lane = lanes_of((ROWS, LANES))
    first, second = slice(0, LANES), slice(LANES, wide)
    to_left[0:ROWS, :] = left[0, :, first]
    to_left[ROWS : 2 * ROWS, :] = left[1, :, first]
    far_u = pltpu.roll(left[0, :, second], 96, 1)
    far_h = pltpu.roll(left[1, :, second], 112, 1)
    to_left[2 * ROWS : 3 * ROWS, :] = jnp.where(
        lane < 96, left[2, :, first], jnp.where(lane < 112, far_u, far_h)
    )
    to_right[0:ROWS, :] = right[0, :, second]
    to_right[ROWS : 2 * ROWS, :] = right[1, :, second]
    far_u = pltpu.roll(right[0, :, first], 16, 1)
    far_h = pltpu.roll(right[1, :, first], 32, 1)
    to_right[2 * ROWS : 3 * ROWS, :] = jnp.where(
        lane >= 32, right[2, :, second], jnp.where(lane < 16, far_u, far_h)
    )


def pack_y(u, h, a):
    shape = jax.ShapeDtypeStruct((3 * ROWS, LANES), F32)
    rows = jax.ShapeDtypeStruct((8, WIDE), F32)
    return pl.pallas_call(
        pack_y_kernel,
        out_shape=(shape, shape, rows, rows),
        in_specs=[HBM] * 3,
        out_specs=[VMEM] * 4,
        scratch_shapes=[
            pltpu.VMEM((3, ROWS, 2 * LANES), F32),
            pltpu.VMEM((3, ROWS, 2 * LANES), F32),
            pltpu.VMEM((2, 3, 8, COLS), F32),
            pltpu.SemaphoreType.DMA((12,)),
        ],
        compiler_params=whole_grant(500 * 2**10),
    )(u, h, a)


def side_tiles(from_left, from_right, lo, n):
    lane = lanes_of((n, LANES))
    rows = [slice(f * ROWS + lo, f * ROWS + lo + n) for f in range(3)]
    zero = jnp.zeros((n, LANES), F32)
    gy = lax.axis_index("gy")
    lefts = [jnp.where(gy > 0, from_left[r, :], zero) for r in rows]
    rights = [jnp.where(gy < lax.axis_size("gy") - 1, from_right[r, :], zero) for r in rows]
    lx, rx = lefts[2], rights[2]

    def far(left_shift, right_shift):
        return jnp.where(
            lane < 16,
            pltpu.roll(rx, right_shift, 1),
            jnp.where(lane >= 112, pltpu.roll(lx, left_shift, 1), zero),
        )

    return (
        (far(112, 32), lefts[0], rights[0]),
        (far(96, 16), lefts[1], rights[1]),
        (zero, jnp.where(lane >= 32, lx, zero), jnp.where(lane < 96, rx, zero)),
    )


def pack_z_kernel(up_own, down_own, from_left, from_right, up, down, edges, sems):
    pairs = []
    for e, (out, (lo, shifts)) in enumerate(zip((up, down), Z_SHIFTS)):
        sides = side_tiles(from_left, from_right, lo, 8)
        for t in range(3):
            edges[e, :, t * LANES : (t + 1) * LANES] = three_fields([side[t] for side in sides], shifts)
        pairs.append((edges.at[e, :, 0:OWN], out.at[:, 0:OWN]))
        pairs.append((edges.at[e, :, OWN : 3 * LANES], out.at[:, OWN + COLS : WIDE]))
    for copy in start_all(pairs, sems):
        copy.wait()


def pack_z(up_own, down_own, from_left, from_right):
    shape = jax.ShapeDtypeStruct((8, WIDE), F32)
    return pl.pallas_call(
        pack_z_kernel,
        out_shape=(shape, shape),
        in_specs=[HBM, HBM, VMEM, VMEM],
        out_specs=(HBM, HBM),
        input_output_aliases={0: 0, 1: 1},
        scratch_shapes=[pltpu.VMEM((2, 8, 3 * LANES), F32), pltpu.SemaphoreType.DMA((4,))],
        compiler_params=whole_grant(200 * 2**10),
    )(up_own, down_own, from_left, from_right)


def table_kernel(times, keeper, table):
    first = lax.axis_index("gz") * (ROWS // LIFT)
    lane = lanes_of((ROWS, LANES))
    solid = []
    for r in range(ROWS // LIFT):
        age = 2400.0 - jnp.full((LIFT, LANES), times[first + r], jnp.int32).astype(F32)
        solid.append(jnp.sqrt(600.0 / age) + 0.2)
    solid = jnp.concatenate(solid, axis=0)
    owners, slots = [], []
    positions = jnp.transpose(keeper[...])
    for j in range(TILES):
        owner, slot = split_position(jnp.broadcast_to(positions[:, j : j + 1], (ROWS, LANES)))
        owners.append(jnp.where(owner == lane, 1.0, 0.0))
        slots.append(jnp.where(slot == lane, solid, 0.0))
    table[...] = lax.dot_general(
        jnp.concatenate(owners, axis=0),
        jnp.concatenate(slots, axis=0),
        (((0,), (0,)), ((), ())),
        precision=lax.Precision.HIGHEST,
        preferred_element_type=F32,
    )


def solid_table(times, keeper):
    return pl.pallas_call(
        table_kernel,
        out_shape=jax.ShapeDtypeStruct((LANES, LANES), F32),
        in_specs=[SMEM, VMEM],
        out_specs=VMEM,
        compiler_params=whole_grant(600 * 2**10),
    )(times, keeper)


def sweep_kernel(
    keeper,
    tally,
    u_in,
    h_in,
    a_in,
    left_hbm,
    right_hbm,
    above_hbm,
    below_hbm,
    table_hbm,
    t_hbm,
    h_hbm,
    m_hbm,
    send_hbm,
    u_first,
    h_first,
    a_wide,
    fields,
    phi_buf,
    load_buf,
    tally_buf,
    t_out,
    h_out,
    m_out,
    send,
    from_left,
    from_right,
    above,
    below,
    table,
    sems,
):
    gz, gy = lax.axis_index("gz"), lax.axis_index("gy")
    last_z, last_y = lax.axis_size("gz") - 1, lax.axis_size("gy") - 1
    tiles = ROWS // 8 + 1

    own_cells = (slice(0, ROWS), slice(OWN, OWN + COLS))
    pairs = [(src, wide.at[own_cells]) for src, wide in ((u_in, u_first), (h_in, h_first), (a_in, a_wide))]
    pairs += [(left_hbm, from_left), (right_hbm, from_right), (above_hbm, above), (below_hbm, below)]
    pairs += [(table_hbm, table)]
    loads = start_all(pairs, sems)

    send[...] = jnp.zeros_like(send)
    for copy in loads:
        copy.wait()
    for o in range(LANES):
        send[o * SEND + AGE_ROW : o * SEND + AGE_ROW + 1, :] = table[o : o + 1, :]

    sides = side_tiles(from_left, from_right, 0, ROWS)
    for wide, side in zip((u_first, h_first, a_wide), sides):
        wide[0:ROWS, 0:LANES] = side[0]
        wide[0:ROWS, LANES:OWN] = side[1]
        wide[0:ROWS, OWN + COLS : WIDE] = side[2]
    row8 = lax.broadcasted_iota(jnp.int32, (8, WIDE), 0)
    zero = jnp.zeros((8, WIDE), F32)
    top, bottom = jnp.where(gz > 0, above[...], zero), jnp.where(gz < last_z, below[...], zero)
    for wide, down_shift, up_shift in ((u_first, 0, 5), (h_first, 5, 2), (a_wide, 2, 0)):
        b = pltpu.roll(bottom, down_shift, 0) if down_shift else bottom
        t = pltpu.roll(top, up_shift, 0) if up_shift else top
        wide[ROWS : ROWS + 8, :] = jnp.where(row8 < 3, b, jnp.where(row8 >= 5, t, zero))

    column = lanes_of((8, WIDE))
    line = lax.rem(column + (16 * NX - OWN), NX)
    not_first, not_last = line != 0, line != NX - 1
    on_left = (column >= 64) & (column < OWN)
    on_own = (column >= OWN) & (column < OWN + COLS)
    left_is, right_is = (gy > 0).astype(jnp.int32), (gy < last_y).astype(jnp.int32)
    above_is, below_is = (gz > 0).astype(jnp.int32), (gz < last_z).astype(jnp.int32)
    inside_columns = jnp.where(on_own, 1, jnp.where(on_left, left_is, right_is))

    def fill(r, carry):
        rows = pl.ds(pl.multiple_of(r * 8, 8), 8)
        h = h_first[rows, :]
        fields[0, 0, rows, :] = u_first[rows, :]
        fields[0, 1, rows, :] = h
        fields[0, 2, rows, :] = excess_diffusivity(h)
        for f in range(3):
            fields[1, f, rows, 0:LANES] = jnp.zeros((8, LANES), F32)
        return carry

    lax.fori_loop(0, tiles, fill, 0, unroll=True)

    def step(src, r):
        here = pl.ds(pl.multiple_of(r * 8, 8), 8)
        before = pl.ds(pl.multiple_of(jnp.where(r == 0, tiles - 1, r - 1) * 8, 8), 8)
        after = pl.ds(pl.multiple_of(jnp.where(r == tiles - 1, 0, r + 1) * 8, 8), 8)

        def around(f):
            v = fields[src, f, here, :]
            lower, upper = fields[src, f, before, :], fields[src, f, after, :]
            return (
                pltpu.roll(jnp.where(row8 == 0, upper, v), 7, 0),
                pltpu.roll(jnp.where(row8 == 7, lower, v), 1, 0),
                pltpu.roll(v, WIDE - NX, 1),
                pltpu.roll(v, NX, 1),
                pltpu.roll(jnp.where(not_first, v, 0.0), WIDE - 1, 1),
                pltpu.roll(jnp.where(not_last, v, 0.0), 1, 1),
            )

        u, h, d = fields[src, 0, here, :], fields[src, 1, here, :], fields[src, 2, here, :]
        r_now = rate_of(u, h, a_wide[here, :])
        u_next = (u_first[here, :] + 4.0 * r_now + sum(around(0))) * (1.0 / 7.0)
        hs, ds = around(1), around(2)
        conduct = 3.0 * (d + 2.0 * D0) + 0.5 * sum(ds)
        inflow = 0.5 * ((d + 2.0 * D0) * sum(hs) + sum(x * y for x, y in zip(ds, hs)))
        h_next = (h_first[here, :] - 0.5 * r_now + inflow) / (1.0 + conduct)
        return u_next, h_next

    def middle(src):
        def run(r, carry):
            rows = pl.ds(pl.multiple_of(r * 8, 8), 8)
            u, h = step(src, r)
            own_rows = (r < tiles - 1).astype(jnp.int32)
            below_in, above_in = jnp.maximum(own_rows, below_is), jnp.maximum(own_rows, above_is)
            keep = inside_columns * jnp.where(row8 < 4, below_in, above_in) > 0
            u, h = jnp.where(keep, u, 0.0), jnp.where(keep, h, 0.0)
            d = excess_diffusivity(h)
            for f, v in enumerate((u, h, d)):
                fields[1 - src, f, rows, LANES:WIDE] = v[:, LANES:WIDE]
            return carry

        lax.fori_loop(0, tiles, run, 0, unroll=True)

    middle(0)
    middle(1)

    lane8 = lanes_of((8, LANES))

    counts_t = jnp.transpose(tally[...])
    for r in range(tiles - 1):
        tally_buf[r * 8 : (r + 1) * 8, 0:TILES] = counts_t[r * 8 : (r + 1) * 8, :]

    def last(r, carry):
        rows = pl.ds(pl.multiple_of(r * 8, 8), 8)
        u, h = step(0, r)
        u, h = u[:, OWN : OWN + COLS], h[:, OWN : OWN + COLS]
        a = a_wide[rows, OWN : OWN + COLS]
        m = a + rate_of(u, h, a)
        t_out[rows, :] = u
        h_out[rows, :] = h
        m_out[rows, :] = m
        load = -m * (0.075 * u + 0.3 * (1.0 - h))
        phi = jnp.exp(0.3 * u) * (0.1 + 0.9 * h * h)
        counts = tally_buf[rows, :]
        for j in range(TILES):
            part = slice(j * LANES, (j + 1) * LANES)
            placed = lane8 < jnp.broadcast_to(counts[:, j : j + 1], (8, LANES))
            block_rows = pl.ds(pl.multiple_of(j * ROWS + r * 8, 8), 8)
            phi_buf[block_rows, :] = jnp.where(placed, phi[:, part], 0.0)
            load_buf[block_rows, :] = load[:, part]
        return carry

    lax.fori_loop(0, tiles - 1, last, 0, unroll=True)

    results = start_all([(t_out, t_hbm), (h_out, h_hbm), (m_out, m_hbm)], sems)

    def scatter(z, carry):
        for j in range(TILES):
            at = place_of(keeper[j, z], SEND)
            block = pl.ds(j * ROWS + z, 1)
            send[pl.ds(at, 1), :] = phi_buf[block, :]
            send[pl.ds(at + CAP, 1), :] = load_buf[block, :]
        return carry

    lax.fori_loop(0, ROWS, scatter, 0)
    message = pltpu.make_async_copy(send, send_hbm, sems.at[3])
    message.start()
    for copy in results:
        copy.wait()
    message.wait()


def sweeps(keeper, tally, u, h, a, from_left, from_right, above, below, table):
    grid_shape = jax.ShapeDtypeStruct((ROWS, COLS), F32)
    wide = pltpu.VMEM((ROWS + 8, WIDE), F32)
    return pl.pallas_call(
        sweep_kernel,
        out_shape=(grid_shape, grid_shape, grid_shape, jax.ShapeDtypeStruct((LANES * SEND, LANES), F32)),
        in_specs=[SMEM, VMEM] + [HBM] * 8,
        out_specs=[HBM] * 4,
        scratch_shapes=[
            wide,
            wide,
            wide,
            pltpu.VMEM((2, 3, ROWS + 8, WIDE), F32),
            pltpu.VMEM((TILES * ROWS, LANES), F32),
            pltpu.VMEM((TILES * ROWS, LANES), F32),
            pltpu.VMEM((ROWS, LANES), jnp.int32),
            pltpu.VMEM((ROWS, COLS), F32),
            pltpu.VMEM((ROWS, COLS), F32),
            pltpu.VMEM((ROWS, COLS), F32),
            pltpu.VMEM((LANES * SEND, LANES), F32),
            pltpu.VMEM((3 * ROWS, LANES), F32),
            pltpu.VMEM((3 * ROWS, LANES), F32),
            pltpu.VMEM((8, WIDE), F32),
            pltpu.VMEM((8, WIDE), F32),
            pltpu.VMEM((LANES, LANES), F32),
            pltpu.SemaphoreType.DMA((8,)),
        ],
        compiler_params=whole_grant(400 * 2**10),
    )(keeper, tally, u, h, a, from_left, from_right, above, below, table)


GROUP = 16
PAD = 16
UNROLL = 4
PARTS = LANES // GROUP


def decay_rates():
    unit = lax.broadcasted_iota(jnp.int32, (UNITS, LANES), 0)
    scale = jnp.zeros((UNITS, LANES), F32)
    for m in range(UNITS):
        scale = jnp.where(unit == m, -math.log2(math.e) / (0.1 * 3.0**m), scale)
    return scale


def unit_change(prior, got, at, scale):
    phi = jnp.broadcast_to(got[pl.ds(at, 1), :], (UNITS, LANES))
    load = jnp.broadcast_to(got[pl.ds(at + CAP, 1), :], (UNITS, LANES))
    return (1.0 - jnp.exp2(phi * scale)) * (load - prior)


def sum_units(parts):
    row = lax.broadcasted_iota(jnp.int32, (8, LANES), 0)
    low = row < 4
    pairs = []
    for k in range(4):
        x, y = parts[k], parts[k + 4]
        pairs.append(jnp.where(low, x, y) + pltpu.roll(jnp.where(low, y, x), 4, 0))
    for step in (2, 1):
        first = (row & step) == 0
        pairs = [
            jnp.where(
                first,
                pairs[k] + pltpu.roll(pairs[k], 8 - step, 0),
                pairs[k + step] + pltpu.roll(pairs[k + step], step, 0),
            )
            for k in range(step)
        ]
    return pairs[0]


def load_states(got_hbm, chain_hbm, tension_hbm, got, chain, tension, sems):
    pairs = [(tension_hbm, tension.at[0 : LANES * CAP])]
    for i in range(PARTS):
        for rows, src, dst in ((GROUP * SEND, got_hbm, got), (GROUP * CAP, chain_hbm, chain)):
            part = slice(i * rows, (i + 1) * rows)
            pairs.append((src.at[part], dst.at[part]))
    return start_all(pairs, sems)


def creep_kernel(got_hbm, chain_hbm, tension_hbm, creep_hbm, got, chain, tension, creep, in_sems, out_sems):
    tension[LANES * CAP :, :] = jnp.ones((PAD, LANES), F32)
    loads = load_states(got_hbm, chain_hbm, tension_hbm, got, chain, tension, in_sems)
    scale = decay_rates()
    diagonal = lanes_of((16, LANES)) == lax.broadcasted_iota(jnp.int32, (16, LANES), 0)

    def one(s, carry):
        base = s * SEND
        ages = jnp.broadcast_to(got[pl.ds(base + AGE_ROW, 1), :], (16, LANES))
        solid = jnp.sum(jnp.where(diagonal, ages, 0.0), axis=1, keepdims=True)
        zero = jnp.zeros((UNITS, LANES), F32)
        changes = [unit_change(chain[s * CAP + k], got, base + k, scale) for k in range(CAP)]
        changes += [zero] * (16 - CAP)
        total = jnp.concatenate([sum_units(changes[:8]), sum_units(changes[8:])], axis=0)
        rows = pl.ds(s * CAP, 16)
        phi, load = got[pl.ds(base, 16), :], got[pl.ds(base + CAP - 1, 16), :]
        load = pltpu.roll(load, 15, 0)
        before = tension[rows, :]
        after = before / (1.0 + 0.2 * phi * before)
        creep[rows, :] = solid * total + (0.1 / 0.15) * phi * after * load
        return carry

    loads[0].wait()
    stores = []
    for i in range(PARTS):
        for copy in loads[1 + 2 * i : 3 + 2 * i]:
            copy.wait()
        lax.fori_loop(i * GROUP, (i + 1) * GROUP, one, 0, unroll=UNROLL)
        part = slice(i * GROUP * BACK, (i + 1) * GROUP * BACK)
        stores.append(pltpu.make_async_copy(creep.at[part], creep_hbm.at[part], out_sems.at[i]))
        stores[-1].start()
    for copy in stores:
        copy.wait()


def state_kernel(
    got_hbm, chain_hbm, tension_hbm, chain_new, tension_new, got, chain, tension, in_sems, out_sems
):
    tension[LANES * CAP :, :] = jnp.ones((PAD, LANES), F32)
    loads = load_states(got_hbm, chain_hbm, tension_hbm, got, chain, tension, in_sems)
    scale = decay_rates()
    used = lax.broadcasted_iota(jnp.int32, (16, LANES), 0) < CAP

    def one(s, carry):
        base = s * SEND
        for k in range(CAP):
            prior = chain[s * CAP + k]
            chain[s * CAP + k] = prior + unit_change(prior, got, base + k, scale)
        phi = got[pl.ds(base, 16), :]
        rows = pl.ds(s * CAP, 16)
        before = tension[rows, :]
        tension[rows, :] = jnp.where(used, before / (1.0 + 0.2 * phi * before), before)
        return carry

    loads[0].wait()
    stores = []
    n = GROUP * CAP
    for i in range(PARTS):
        for copy in loads[1 + 2 * i : 3 + 2 * i]:
            copy.wait()
        lax.fori_loop(i * GROUP, (i + 1) * GROUP, one, 0, unroll=2)
        part = slice(i * n, (i + 1) * n)
        stores.append(pltpu.make_async_copy(chain.at[part], chain_new.at[part], out_sems.at[i]))
        stores[-1].start()
    stores.append(pltpu.make_async_copy(tension.at[0 : LANES * CAP], tension_new, out_sems.at[PARTS]))
    stores[-1].start()
    for copy in stores:
        copy.wait()


def owner_scratch(creep):
    return [
        pltpu.VMEM((LANES * SEND, LANES), F32),
        pltpu.VMEM((LANES * CAP, UNITS, LANES), F32),
        pltpu.VMEM((LANES * CAP + PAD, LANES), F32),
        *creep,
        pltpu.SemaphoreType.DMA((2 * PARTS + 1,)),
        pltpu.SemaphoreType.DMA((PARTS + 1,)),
    ]


def creep_of(got, chain, tension):
    shape = (LANES * BACK, LANES)
    return pl.pallas_call(
        creep_kernel,
        out_shape=jax.ShapeDtypeStruct(shape, F32),
        in_specs=[HBM] * 3,
        out_specs=HBM,
        scratch_shapes=owner_scratch([pltpu.VMEM((LANES * CAP + PAD, LANES), F32)]),
        compiler_params=whole_grant(600 * 2**10),
        cost_estimate=pl.CostEstimate(flops=20 * chain.size, bytes_accessed=4 * chain.size, transcendentals=chain.size),
    )(got, chain, tension)


def states_of(got, chain, tension):
    return pl.pallas_call(
        state_kernel,
        out_shape=(jax.ShapeDtypeStruct(chain.shape, F32), jax.ShapeDtypeStruct(tension.shape, F32)),
        in_specs=[HBM] * 3,
        out_specs=(HBM, HBM),
        scratch_shapes=owner_scratch([]),
        compiler_params=whole_grant(600 * 2**10),
        cost_estimate=pl.CostEstimate(flops=20 * chain.size, bytes_accessed=8 * chain.size, transcendentals=chain.size),
    )(got, chain, tension)


def collect_kernel(keeper, back, out, blocks):
    def line(z, carry):
        for j in range(TILES):
            at = place_of(keeper[j, z], BACK)
            blocks[pl.ds(j * ROWS + z, 1), :] = back[pl.ds(at, 1), :]
        return carry

    lax.fori_loop(0, ROWS, line, 0, unroll=4)
    for j in range(TILES):
        out[:, j * LANES : (j + 1) * LANES] = blocks[j * ROWS : (j + 1) * ROWS, :]


def collect(keeper, back):
    return pl.pallas_call(
        collect_kernel,
        out_shape=jax.ShapeDtypeStruct((ROWS, COLS), F32),
        in_specs=[SMEM, VMEM],
        out_specs=VMEM,
        scratch_shapes=[pltpu.VMEM((TILES * ROWS, LANES), F32)],
        compiler_params=grant(4),
    )(keeper, back)


def both_ways(axis, to_lower, to_higher):
    count = lax.axis_size(axis)
    from_lower = lax.ppermute(to_higher, axis, [(i, (i + 1) % count) for i in range(count)])
    from_higher = lax.ppermute(to_lower, axis, [((i + 1) % count, i) for i in range(count)])
    return from_lower, from_higher


def exchange(x):
    flat = x.reshape(LANES, 1, -1)
    return lax.all_to_all(flat, ("gz", "gy"), split_axis=0, concat_axis=0, tiled=True).reshape(x.shape)


def body(u, h, a, tally, keeper, times, chain, tension):
    tally, keeper = tally.T, keeper.T
    to_left, to_right, up_own, down_own = pack_y(u, h, a)
    from_left, from_right = both_ways("gy", to_left, to_right)
    table = solid_table(times, keeper)
    up_own, down_own, table = lax.optimization_barrier((up_own, down_own, table))
    up, down = pack_z(up_own, down_own, from_left, from_right)
    above, below = both_ways("gz", up, down)
    t_new, h_new, m_new, send = sweeps(keeper, tally, u, h, a, from_left, from_right, above, below, table)
    got = exchange(send)
    creep = creep_of(got, chain, tension)
    back = exchange(creep)
    chain_new, tension_new = states_of(got, chain, tension)
    return t_new, h_new, m_new, collect(keeper, back), chain_new, tension_new


def solution(mesh):
    grid = P("gz", "gy")
    owners = ("gz", "gy")
    return jax.shard_map(
        body,
        mesh=mesh,
        in_specs=(grid, grid, grid, grid, grid, P(), P(owners, None, None), P(owners, None)),
        out_specs=(grid, grid, grid, grid, P(owners, None, None), P(owners, None)),
        check_vma=False,
    )
```

```python
import functools
import math

import jax
import jax.numpy as jnp
from jax import lax
from jax.experimental import pallas as pl
from jax.experimental.pallas import tpu as pltpu
from jax.sharding import PartitionSpec as P

NX = 48
LANES = 128
LIFT = 8
CAP = 14
UNITS = 8
ROWS = 48
TILES = 12
COLS = TILES * LANES
WIDE = (TILES + 3) * LANES
OWN = 2 * LANES
SEND = 2 * CAP + 1
BACK = CAP
AGE_ROW = 2 * CAP

D0 = 0.05 + 0.95 / (1.0 + 5.0**16)

F32 = jnp.float32


def grant(mib):
    return pltpu.CompilerParams(vmem_limit_bytes=mib * 2**20)


def whole_grant(room):
    return pltpu.CompilerParams(vmem_limit_bytes=64 * 2**20 - room)


HBM = pl.BlockSpec(memory_space=pltpu.HBM)
VMEM = pl.BlockSpec(memory_space=pltpu.VMEM)
SMEM = pl.BlockSpec(memory_space=pltpu.SMEM)


def rate_of(u, h, a):
    q = 7.5 - 7.5 * h
    q = q * q
    return 0.05 * (1.0 - a) * jnp.exp(0.5 * u) / (1.0 + q * q)


def excess_diffusivity(h):
    p = 5.0 * (1.0 - h)
    p = p * p
    p = p * p
    p = p * p
    p = p * p
    return (0.05 - D0) + 0.95 / (1.0 + p)


def lanes_of(shape):
    return lax.broadcasted_iota(jnp.int32, shape, len(shape) - 1)


def split_position(p):
    owner = lax.shift_right_logical(p * 37450, 19)
    return owner, p - CAP * owner


def place_of(p, stride):
    return p + (stride - CAP) * lax.shift_right_logical(p * 37450, 19)


def start_all(pairs, sems):
    copies = [pltpu.make_async_copy(src, dst, sems.at[i]) for i, (src, dst) in enumerate(pairs)]
    for copy in copies:
        copy.start()
    return copies


Z_SHIFTS = ((0, (0, 3, 6)), (ROWS - 8, (3, 6, 0)))


def three_fields(fields, shifts):
    u, h, a = [pltpu.roll(v, s, 0) if s else v for v, s in zip(fields, shifts)]
    row = lax.broadcasted_iota(jnp.int32, u.shape, 0)
    return jnp.where(row < 3, u, jnp.where(row < 6, h, a))


def pack_y_kernel(u, h, a, to_left, to_right, own, left, right, ends, sems):
    wide = 2 * LANES
    pairs = []
    for f, field in enumerate((u, h, a)):
        pairs.append((field.at[:, 0:wide], left.at[f]))
        pairs.append((field.at[:, COLS - wide : COLS], right.at[f]))
        pairs.append((field.at[0:8, :], ends.at[0, f]))
        pairs.append((field.at[ROWS - 8 : ROWS, :], ends.at[1, f]))
    for copy in start_all(pairs, sems):
        copy.wait()
    for e, (_, shifts) in enumerate(Z_SHIFTS):
        own[8 * e : 8 * e + 8, :] = three_fields([ends[e, f] for f in range(3)], shifts)
    lane = lanes_of((ROWS, LANES))
    first, second = slice(0, LANES), slice(LANES, wide)
    to_left[0:ROWS, :] = left[0, :, first]
    to_left[ROWS : 2 * ROWS, :] = left[1, :, first]
    far_u = pltpu.roll(left[0, :, second], 96, 1)
    far_h = pltpu.roll(left[1, :, second], 112, 1)
    to_left[2 * ROWS : 3 * ROWS, :] = jnp.where(
        lane < 96, left[2, :, first], jnp.where(lane < 112, far_u, far_h)
    )
    to_right[0:ROWS, :] = right[0, :, second]
    to_right[ROWS : 2 * ROWS, :] = right[1, :, second]
    far_u = pltpu.roll(right[0, :, first], 16, 1)
    far_h = pltpu.roll(right[1, :, first], 32, 1)
    to_right[2 * ROWS : 3 * ROWS, :] = jnp.where(
        lane >= 32, right[2, :, second], jnp.where(lane < 16, far_u, far_h)
    )


def pack_y(u, h, a):
    shape = jax.ShapeDtypeStruct((3 * ROWS, LANES), F32)
    rows = jax.ShapeDtypeStruct((16, COLS), F32)
    return pl.pallas_call(
        pack_y_kernel,
        out_shape=(shape, shape, rows),
        in_specs=[HBM] * 3,
        out_specs=[VMEM] * 3,
        scratch_shapes=[
            pltpu.VMEM((3, ROWS, 2 * LANES), F32),
            pltpu.VMEM((3, ROWS, 2 * LANES), F32),
            pltpu.VMEM((2, 3, 8, COLS), F32),
            pltpu.SemaphoreType.DMA((12,)),
        ],
        compiler_params=whole_grant(500 * 2**10),
    )(u, h, a)


def side_tiles(from_left, from_right, lo, n):
    lane = lanes_of((n, LANES))
    rows = [slice(f * ROWS + lo, f * ROWS + lo + n) for f in range(3)]
    zero = jnp.zeros((n, LANES), F32)
    gy = lax.axis_index("gy")
    lefts = [jnp.where(gy > 0, from_left[r, :], zero) for r in rows]
    rights = [jnp.where(gy < lax.axis_size("gy") - 1, from_right[r, :], zero) for r in rows]
    lx, rx = lefts[2], rights[2]

    def far(left_shift, right_shift):
        return jnp.where(
            lane < 16,
            pltpu.roll(rx, right_shift, 1),
            jnp.where(lane >= 112, pltpu.roll(lx, left_shift, 1), zero),
        )

    return (
        (far(112, 32), lefts[0], rights[0]),
        (far(96, 16), lefts[1], rights[1]),
        (zero, jnp.where(lane >= 32, lx, zero), jnp.where(lane < 96, rx, zero)),
    )


def pack_z_kernel(own, from_left, from_right, up, down):
    for e, (out, (lo, shifts)) in enumerate(zip((up, down), Z_SHIFTS)):
        sides = side_tiles(from_left, from_right, lo, 8)
        out[:, OWN : OWN + COLS] = own[8 * e : 8 * e + 8, :]
        for t, at in enumerate((0, LANES, OWN + COLS)):
            out[:, at : at + LANES] = three_fields([side[t] for side in sides], shifts)


def pack_z(own, from_left, from_right):
    shape = jax.ShapeDtypeStruct((8, WIDE), F32)
    return pl.pallas_call(
        pack_z_kernel,
        out_shape=(shape, shape),
        in_specs=[VMEM] * 3,
        out_specs=(VMEM, VMEM),
        compiler_params=grant(4),
    )(own, from_left, from_right)


def table_kernel(times, keeper, table):
    first = lax.axis_index("gz") * (ROWS // LIFT)
    lane = lanes_of((ROWS, LANES))
    solid = []
    for r in range(ROWS // LIFT):
        age = 2400.0 - jnp.full((LIFT, LANES), times[first + r], jnp.int32).astype(F32)
        solid.append(jnp.sqrt(600.0 / age) + 0.2)
    solid = jnp.concatenate(solid, axis=0)
    owners, slots = [], []
    positions = jnp.transpose(keeper[...])
    for j in range(TILES):
        owner, slot = split_position(jnp.broadcast_to(positions[:, j : j + 1], (ROWS, LANES)))
        owners.append(jnp.where(owner == lane, 1.0, 0.0))
        slots.append(jnp.where(slot == lane, solid, 0.0))
    table[...] = lax.dot_general(
        jnp.concatenate(owners, axis=0),
        jnp.concatenate(slots, axis=0),
        (((0,), (0,)), ((), ())),
        precision=lax.Precision.HIGHEST,
        preferred_element_type=F32,
    )


def solid_table(times, keeper):
    return pl.pallas_call(
        table_kernel,
        out_shape=jax.ShapeDtypeStruct((LANES, LANES), F32),
        in_specs=[SMEM, VMEM],
        out_specs=VMEM,
        compiler_params=whole_grant(600 * 2**10),
    )(times, keeper)


def sweep_kernel(
    keeper,
    tally,
    u_in,
    h_in,
    a_in,
    left_hbm,
    right_hbm,
    above_hbm,
    below_hbm,
    table_hbm,
    t_hbm,
    h_hbm,
    m_hbm,
    send_hbm,
    u_first,
    h_first,
    a_wide,
    fields,
    phi_buf,
    load_buf,
    tally_buf,
    t_out,
    h_out,
    m_out,
    send,
    from_left,
    from_right,
    above,
    below,
    table,
    sems,
):
    gz, gy = lax.axis_index("gz"), lax.axis_index("gy")
    last_z, last_y = lax.axis_size("gz") - 1, lax.axis_size("gy") - 1
    tiles = ROWS // 8 + 1

    own_cells = (slice(0, ROWS), slice(OWN, OWN + COLS))
    pairs = [(src, wide.at[own_cells]) for src, wide in ((u_in, u_first), (h_in, h_first), (a_in, a_wide))]
    pairs += [(left_hbm, from_left), (right_hbm, from_right), (above_hbm, above), (below_hbm, below)]
    pairs += [(table_hbm, table)]
    loads = start_all(pairs, sems)

    send[...] = jnp.zeros_like(send)
    for copy in loads:
        copy.wait()
    for o in range(LANES):
        send[o * SEND + AGE_ROW : o * SEND + AGE_ROW + 1, :] = table[o : o + 1, :]

    sides = side_tiles(from_left, from_right, 0, ROWS)
    for wide, side in zip((u_first, h_first, a_wide), sides):
        wide[0:ROWS, 0:LANES] = side[0]
        wide[0:ROWS, LANES:OWN] = side[1]
        wide[0:ROWS, OWN + COLS : WIDE] = side[2]
    row8 = lax.broadcasted_iota(jnp.int32, (8, WIDE), 0)
    zero = jnp.zeros((8, WIDE), F32)
    top, bottom = jnp.where(gz > 0, above[...], zero), jnp.where(gz < last_z, below[...], zero)
    for wide, down_shift, up_shift in ((u_first, 0, 5), (h_first, 5, 2), (a_wide, 2, 0)):
        b = pltpu.roll(bottom, down_shift, 0) if down_shift else bottom
        t = pltpu.roll(top, up_shift, 0) if up_shift else top
        wide[ROWS : ROWS + 8, :] = jnp.where(row8 < 3, b, jnp.where(row8 >= 5, t, zero))

    column = lanes_of((8, WIDE))
    line = lax.rem(column + (16 * NX - OWN), NX)
    not_first, not_last = line != 0, line != NX - 1
    on_left = (column >= 64) & (column < OWN)
    on_own = (column >= OWN) & (column < OWN + COLS)
    left_is, right_is = (gy > 0).astype(jnp.int32), (gy < last_y).astype(jnp.int32)
    above_is, below_is = (gz > 0).astype(jnp.int32), (gz < last_z).astype(jnp.int32)
    inside_columns = jnp.where(on_own, 1, jnp.where(on_left, left_is, right_is))

    def fill(r, carry):
        rows = pl.ds(pl.multiple_of(r * 8, 8), 8)
        h = h_first[rows, :]
        fields[0, 0, rows, :] = u_first[rows, :]
        fields[0, 1, rows, :] = h
        fields[0, 2, rows, :] = excess_diffusivity(h)
        for f in range(3):
            fields[1, f, rows, 0:LANES] = jnp.zeros((8, LANES), F32)
        return carry

    lax.fori_loop(0, tiles, fill, 0, unroll=True)

    def step(src, r):
        here = pl.ds(pl.multiple_of(r * 8, 8), 8)
        before = pl.ds(pl.multiple_of(jnp.where(r == 0, tiles - 1, r - 1) * 8, 8), 8)
        after = pl.ds(pl.multiple_of(jnp.where(r == tiles - 1, 0, r + 1) * 8, 8), 8)

        def around(f):
            v = fields[src, f, here, :]
            lower, upper = fields[src, f, before, :], fields[src, f, after, :]
            return (
                pltpu.roll(jnp.where(row8 == 0, upper, v), 7, 0),
                pltpu.roll(jnp.where(row8 == 7, lower, v), 1, 0),
                pltpu.roll(v, WIDE - NX, 1),
                pltpu.roll(v, NX, 1),
                pltpu.roll(jnp.where(not_first, v, 0.0), WIDE - 1, 1),
                pltpu.roll(jnp.where(not_last, v, 0.0), 1, 1),
            )

        u, h, d = fields[src, 0, here, :], fields[src, 1, here, :], fields[src, 2, here, :]
        r_now = rate_of(u, h, a_wide[here, :])
        u_next = (u_first[here, :] + 4.0 * r_now + sum(around(0))) * (1.0 / 7.0)
        hs, ds = around(1), around(2)
        conduct = 3.0 * (d + 2.0 * D0) + 0.5 * sum(ds)
        inflow = 0.5 * ((d + 2.0 * D0) * sum(hs) + sum(x * y for x, y in zip(ds, hs)))
        h_next = (h_first[here, :] - 0.5 * r_now + inflow) / (1.0 + conduct)
        return u_next, h_next

    def middle(src):
        def run(r, carry):
            rows = pl.ds(pl.multiple_of(r * 8, 8), 8)
            u, h = step(src, r)
            own_rows = (r < tiles - 1).astype(jnp.int32)
            below_in, above_in = jnp.maximum(own_rows, below_is), jnp.maximum(own_rows, above_is)
            keep = inside_columns * jnp.where(row8 < 4, below_in, above_in) > 0
            u, h = jnp.where(keep, u, 0.0), jnp.where(keep, h, 0.0)
            d = excess_diffusivity(h)
            for f, v in enumerate((u, h, d)):
                fields[1 - src, f, rows, LANES:WIDE] = v[:, LANES:WIDE]
            return carry

        lax.fori_loop(0, tiles, run, 0, unroll=True)

    middle(0)
    middle(1)

    lane8 = lanes_of((8, LANES))

    counts_t = jnp.transpose(tally[...])
    for r in range(tiles - 1):
        tally_buf[r * 8 : (r + 1) * 8, 0:TILES] = counts_t[r * 8 : (r + 1) * 8, :]

    def last(r, carry):
        rows = pl.ds(pl.multiple_of(r * 8, 8), 8)
        u, h = step(0, r)
        u, h = u[:, OWN : OWN + COLS], h[:, OWN : OWN + COLS]
        a = a_wide[rows, OWN : OWN + COLS]
        m = a + rate_of(u, h, a)
        t_out[rows, :] = u
        h_out[rows, :] = h
        m_out[rows, :] = m
        load = -m * (0.075 * u + 0.3 * (1.0 - h))
        phi = jnp.exp(0.3 * u) * (0.1 + 0.9 * h * h)
        counts = tally_buf[rows, :]
        for j in range(TILES):
            part = slice(j * LANES, (j + 1) * LANES)
            placed = lane8 < jnp.broadcast_to(counts[:, j : j + 1], (8, LANES))
            block_rows = pl.ds(pl.multiple_of(j * ROWS + r * 8, 8), 8)
            phi_buf[block_rows, :] = jnp.where(placed, phi[:, part], 0.0)
            load_buf[block_rows, :] = load[:, part]
        return carry

    lax.fori_loop(0, tiles - 1, last, 0, unroll=True)

    results = start_all([(t_out, t_hbm), (h_out, h_hbm), (m_out, m_hbm)], sems)

    def scatter(z, carry):
        for j in range(TILES):
            at = place_of(keeper[j, z], SEND)
            block = pl.ds(j * ROWS + z, 1)
            send[pl.ds(at, 1), :] = phi_buf[block, :]
            send[pl.ds(at + CAP, 1), :] = load_buf[block, :]
        return carry

    lax.fori_loop(0, ROWS, scatter, 0)
    message = pltpu.make_async_copy(send, send_hbm, sems.at[3])
    message.start()
    for copy in results:
        copy.wait()
    message.wait()


def sweeps(keeper, tally, u, h, a, from_left, from_right, above, below, table):
    grid_shape = jax.ShapeDtypeStruct((ROWS, COLS), F32)
    wide = pltpu.VMEM((ROWS + 8, WIDE), F32)
    return pl.pallas_call(
        sweep_kernel,
        out_shape=(grid_shape, grid_shape, grid_shape, jax.ShapeDtypeStruct((LANES * SEND, LANES), F32)),
        in_specs=[SMEM, VMEM] + [HBM] * 8,
        out_specs=[HBM] * 4,
        scratch_shapes=[
            wide,
            wide,
            wide,
            pltpu.VMEM((2, 3, ROWS + 8, WIDE), F32),
            pltpu.VMEM((TILES * ROWS, LANES), F32),
            pltpu.VMEM((TILES * ROWS, LANES), F32),
            pltpu.VMEM((ROWS, LANES), jnp.int32),
            pltpu.VMEM((ROWS, COLS), F32),
            pltpu.VMEM((ROWS, COLS), F32),
            pltpu.VMEM((ROWS, COLS), F32),
            pltpu.VMEM((LANES * SEND, LANES), F32),
            pltpu.VMEM((3 * ROWS, LANES), F32),
            pltpu.VMEM((3 * ROWS, LANES), F32),
            pltpu.VMEM((8, WIDE), F32),
            pltpu.VMEM((8, WIDE), F32),
            pltpu.VMEM((LANES, LANES), F32),
            pltpu.SemaphoreType.DMA((8,)),
        ],
        compiler_params=whole_grant(400 * 2**10),
    )(keeper, tally, u, h, a, from_left, from_right, above, below, table)


GROUP = 16
PAD = 16
UNROLL = 4
PARTS = LANES // GROUP


def decay_rates():
    unit = lax.broadcasted_iota(jnp.int32, (UNITS, LANES), 0)
    scale = jnp.zeros((UNITS, LANES), F32)
    for m in range(UNITS):
        scale = jnp.where(unit == m, -math.log2(math.e) / (0.1 * 3.0**m), scale)
    return scale


def unit_change(prior, got, at, scale):
    phi = jnp.broadcast_to(got[pl.ds(at, 1), :], (UNITS, LANES))
    load = jnp.broadcast_to(got[pl.ds(at + CAP, 1), :], (UNITS, LANES))
    return (1.0 - jnp.exp2(phi * scale)) * (load - prior)


def sum_units(parts):
    row = lax.broadcasted_iota(jnp.int32, (8, LANES), 0)
    low = row < 4
    pairs = []
    for k in range(4):
        x, y = parts[k], parts[k + 4]
        pairs.append(jnp.where(low, x, y) + pltpu.roll(jnp.where(low, y, x), 4, 0))
    for step in (2, 1):
        first = (row & step) == 0
        pairs = [
            jnp.where(
                first,
                pairs[k] + pltpu.roll(pairs[k], 8 - step, 0),
                pairs[k + step] + pltpu.roll(pairs[k + step], step, 0),
            )
            for k in range(step)
        ]
    return pairs[0]


def load_states(got_hbm, chain_hbm, tension_hbm, got, chain, tension, sems):
    pairs = [(tension_hbm, tension.at[0 : LANES * CAP])]
    for i in range(PARTS):
        for rows, src, dst in ((GROUP * SEND, got_hbm, got), (GROUP * CAP, chain_hbm, chain)):
            part = slice(i * rows, (i + 1) * rows)
            pairs.append((src.at[part], dst.at[part]))
    return start_all(pairs, sems)


def creep_kernel(got_hbm, chain_hbm, tension_hbm, creep_hbm, got, chain, tension, creep, in_sems, out_sems):
    tension[LANES * CAP :, :] = jnp.ones((PAD, LANES), F32)
    loads = load_states(got_hbm, chain_hbm, tension_hbm, got, chain, tension, in_sems)
    scale = decay_rates()
    diagonal = lanes_of((16, LANES)) == lax.broadcasted_iota(jnp.int32, (16, LANES), 0)

    def one(s, carry):
        base = s * SEND
        ages = jnp.broadcast_to(got[pl.ds(base + AGE_ROW, 1), :], (16, LANES))
        solid = jnp.sum(jnp.where(diagonal, ages, 0.0), axis=1, keepdims=True)
        zero = jnp.zeros((UNITS, LANES), F32)
        changes = [unit_change(chain[s * CAP + k], got, base + k, scale) for k in range(CAP)]
        changes += [zero] * (16 - CAP)
        total = jnp.concatenate([sum_units(changes[:8]), sum_units(changes[8:])], axis=0)
        rows = pl.ds(s * CAP, 16)
        phi, load = got[pl.ds(base, 16), :], got[pl.ds(base + CAP - 1, 16), :]
        load = pltpu.roll(load, 15, 0)
        before = tension[rows, :]
        after = before / (1.0 + 0.2 * phi * before)
        creep[rows, :] = solid * total + (0.1 / 0.15) * phi * after * load
        return carry

    loads[0].wait()
    stores = []
    for i in range(PARTS):
        for copy in loads[1 + 2 * i : 3 + 2 * i]:
            copy.wait()
        lax.fori_loop(i * GROUP, (i + 1) * GROUP, one, 0, unroll=UNROLL)
        part = slice(i * GROUP * BACK, (i + 1) * GROUP * BACK)
        stores.append(pltpu.make_async_copy(creep.at[part], creep_hbm.at[part], out_sems.at[i]))
        stores[-1].start()
    for copy in stores:
        copy.wait()


def state_kernel(
    got_hbm, chain_hbm, tension_hbm, chain_new, tension_new, got, chain, tension, in_sems, out_sems
):
    tension[LANES * CAP :, :] = jnp.ones((PAD, LANES), F32)
    loads = load_states(got_hbm, chain_hbm, tension_hbm, got, chain, tension, in_sems)
    scale = decay_rates()
    used = lax.broadcasted_iota(jnp.int32, (16, LANES), 0) < CAP

    def one(s, carry):
        base = s * SEND
        for k in range(CAP):
            prior = chain[s * CAP + k]
            chain[s * CAP + k] = prior + unit_change(prior, got, base + k, scale)
        phi = got[pl.ds(base, 16), :]
        rows = pl.ds(s * CAP, 16)
        before = tension[rows, :]
        tension[rows, :] = jnp.where(used, before / (1.0 + 0.2 * phi * before), before)
        return carry

    loads[0].wait()
    stores = []
    n = GROUP * CAP
    for i in range(PARTS):
        for copy in loads[1 + 2 * i : 3 + 2 * i]:
            copy.wait()
        lax.fori_loop(i * GROUP, (i + 1) * GROUP, one, 0, unroll=2)
        part = slice(i * n, (i + 1) * n)
        stores.append(pltpu.make_async_copy(chain.at[part], chain_new.at[part], out_sems.at[i]))
        stores[-1].start()
    stores.append(pltpu.make_async_copy(tension.at[0 : LANES * CAP], tension_new, out_sems.at[PARTS]))
    stores[-1].start()
    for copy in stores:
        copy.wait()


def owner_scratch(creep):
    return [
        pltpu.VMEM((LANES * SEND, LANES), F32),
        pltpu.VMEM((LANES * CAP, UNITS, LANES), F32),
        pltpu.VMEM((LANES * CAP + PAD, LANES), F32),
        *creep,
        pltpu.SemaphoreType.DMA((2 * PARTS + 1,)),
        pltpu.SemaphoreType.DMA((PARTS + 1,)),
    ]


def creep_of(got, chain, tension):
    shape = (LANES * BACK, LANES)
    return pl.pallas_call(
        creep_kernel,
        out_shape=jax.ShapeDtypeStruct(shape, F32),
        in_specs=[HBM] * 3,
        out_specs=HBM,
        scratch_shapes=owner_scratch([pltpu.VMEM((LANES * CAP + PAD, LANES), F32)]),
        compiler_params=whole_grant(600 * 2**10),
        cost_estimate=pl.CostEstimate(flops=20 * chain.size, bytes_accessed=4 * chain.size, transcendentals=chain.size),
    )(got, chain, tension)


def states_of(got, chain, tension):
    return pl.pallas_call(
        state_kernel,
        out_shape=(jax.ShapeDtypeStruct(chain.shape, F32), jax.ShapeDtypeStruct(tension.shape, F32)),
        in_specs=[HBM] * 3,
        out_specs=(HBM, HBM),
        scratch_shapes=owner_scratch([]),
        compiler_params=whole_grant(600 * 2**10),
        cost_estimate=pl.CostEstimate(flops=20 * chain.size, bytes_accessed=8 * chain.size, transcendentals=chain.size),
    )(got, chain, tension)


def collect_kernel(keeper, back, out, blocks):
    def line(z, carry):
        for j in range(TILES):
            at = place_of(keeper[j, z], BACK)
            blocks[pl.ds(j * ROWS + z, 1), :] = back[pl.ds(at, 1), :]
        return carry

    lax.fori_loop(0, ROWS, line, 0, unroll=4)
    for j in range(TILES):
        out[:, j * LANES : (j + 1) * LANES] = blocks[j * ROWS : (j + 1) * ROWS, :]


def collect(keeper, back):
    return pl.pallas_call(
        collect_kernel,
        out_shape=jax.ShapeDtypeStruct((ROWS, COLS), F32),
        in_specs=[SMEM, VMEM],
        out_specs=VMEM,
        scratch_shapes=[pltpu.VMEM((TILES * ROWS, LANES), F32)],
        compiler_params=grant(4),
    )(keeper, back)


def both_ways(axis, to_lower, to_higher):
    count = lax.axis_size(axis)
    from_lower = lax.ppermute(to_higher, axis, [(i, (i + 1) % count) for i in range(count)])
    from_higher = lax.ppermute(to_lower, axis, [((i + 1) % count, i) for i in range(count)])
    return from_lower, from_higher


def exchange(x):
    flat = x.reshape(LANES, 1, -1)
    return lax.all_to_all(flat, ("gz", "gy"), split_axis=0, concat_axis=0, tiled=True).reshape(x.shape)


def body(u, h, a, tally, keeper, times, chain, tension):
    tally, keeper = tally.T, keeper.T
    to_left, to_right, own = pack_y(u, h, a)
    from_left, from_right = both_ways("gy", to_left, to_right)
    table = solid_table(times, keeper)
    own, table, from_left, from_right = lax.optimization_barrier((own, table, from_left, from_right))
    up, down = pack_z(own, from_left, from_right)
    above, below = both_ways("gz", up, down)
    t_new, h_new, m_new, send = sweeps(keeper, tally, u, h, a, from_left, from_right, above, below, table)
    got = exchange(send)
    creep = creep_of(got, chain, tension)
    back = exchange(creep)
    chain_new, tension_new = states_of(got, chain, tension)
    return t_new, h_new, m_new, collect(keeper, back), chain_new, tension_new


def solution(mesh):
    grid = P("gz", "gy")
    owners = ("gz", "gy")
    return jax.shard_map(
        body,
        mesh=mesh,
        in_specs=(grid, grid, grid, grid, grid, P(), P(owners, None, None), P(owners, None)),
        out_specs=(grid, grid, grid, grid, P(owners, None, None), P(owners, None)),
        check_vma=False,
    )
```
